512 devices in a mesh: seg: 64 (over x_hi, z, core), op: 8 (over y, x_lo).
Axes of the slice: x: 4 (x_hi: 2, x_lo: 2; x = x_hi * 2 + x_lo), y: 4, z: 16, core: 2. Of those that a mesh axis runs over, the one named last changes fastest.
Arguments:
- left_in: bfloat16 [64, 8, 24, 128, 128], P('seg', 'op'), may hold values from -6 to 6
- right_in: bfloat16 [64, 8, 24, 128, 128], P('seg', 'op'), may hold values from -6 to 6
- site_blocks: bfloat16 [128, 96, 128, 128], P('seg', 'op'), may hold values from -0.5 to 0.5
- sectors: int32 [128, 96, 2], P('seg'), may hold values from 0 to 23, as said below
- site_operator: float32 [128, 8, 96], P('seg', 'op'), may hold values from 0.4 to 1.2
- sector_sizes: int32 [24], replicated, may hold values from 32 to 128, as said below
Outputs:
- left_env: bfloat16 [64, 8, 24, 128, 128], P('seg', 'op')
- right_env: bfloat16 [64, 8, 24, 128, 128], P('seg', 'op')
- left_sum: float32 [64, 24, 128, 128], P('seg', 'op')
- right_sum: float32 [64, 24, 128, 128], P('seg', 'op')
The draws below stay inside these ranges and needn't reach their ends.
Inputs may be any that keep to these rules, and one draw needn't show every extreme that they name: `sectors`: in every site each sector is the left sector of exactly four blocks and the right sector of exactly four blocks. `sector_sizes`: some sector has all 128 rows live.
All inputs are finite; a program needn't handle non-finite values.
Results may differ from the reference program's by a relative error of at most 0.015.
Values may be sent and summed in bfloat16 or wider, within the bound.
No kernel may reach another device: no remote copies, remote signals or barrier semaphores. Data moves between devices by JAX's collectives and lax.ppermute only.
A program may use at most 64 MiB of HBM per device.

```python
import jax
import jax.numpy as jnp
from jax import lax

B = 128
NS = 24
NBLK = 96
STEPS = 1
SITES = 128
TERMS = 8
N_SEG = 64


def draw_sectors(key, part):
    key = jax.random.fold_in(key, 11)
    keys = jax.random.split(key, 2 * SITES)
    orders = jax.vmap(lambda single: jax.random.permutation(single, NBLK))(keys)
    orders = orders.reshape(SITES, 2, NBLK) % NS
    return jnp.transpose(orders, (0, 2, 1)).astype(jnp.int32)


def draw_sector_sizes(key, part):
    key = jax.random.fold_in(key, 5)
    first_key, second_key = jax.random.split(key)
    sizes_drawn = jax.random.randint(first_key, (NS,), B // 4, B + 1)
    chosen_one = jax.random.randint(second_key, (), 0, NS)
    sizes_drawn = jnp.where(jnp.arange(NS) == chosen_one, B, sizes_drawn)
    return sizes_drawn.astype(jnp.int32)


def shard_levels(own_key, extent, cuts, low, top_value):
    loudness = 1.0
    for dim, parts in cuts:
        steps = jax.random.uniform(jax.random.fold_in(jax.random.fold_in(own_key, 6), dim), (parts,), jnp.float32, low / len(cuts), top_value / len(cuts))
        loudness = loudness * jnp.repeat(jnp.exp(steps), extent[dim] // parts).reshape((-1,) + (1,) * (len(extent) - 1 - dim))
    return loudness


def centred(own_key, extent, scale, bound, pieces=(), kind=jnp.bfloat16):
    drawn = scale * jax.random.normal(own_key, extent, jnp.float32)
    if pieces:
        drawn = drawn * shard_levels(own_key, extent, pieces, -0.22, 0.18)
    return jnp.clip(drawn, -bound, bound).astype(kind)


def setup_inputs(seed: int = 0) -> dict:
    key_list = jax.random.split(jax.random.key(seed), 7)
    left_in = centred(key_list[0], (N_SEG, TERMS, NS, B, B), 1.0, 6.0, ((0, 64), (1, 8)))
    right_in = centred(key_list[1], (N_SEG, TERMS, NS, B, B), 1.0, 6.0, ((0, 64), (1, 8)))
    site_blocks = centred(key_list[2], (SITES, NBLK, B, B), B ** -0.5, 0.5, ((0, 64), (1, 8)))
    sectors = draw_sectors(jax.random.fold_in(key_list[6], 71), 0)
    site_operator = jnp.clip(0.4 + 0.800000042 * jax.random.uniform(key_list[4], (SITES, TERMS, NBLK), jnp.float32) ** shard_levels(key_list[4], (SITES, TERMS, NBLK), ((0, 64), (1, 8)), -0.2, 0.2), 0.4, 1.2)
    sector_sizes = draw_sector_sizes(jax.random.fold_in(key_list[6], 71), 0)
    return dict(left_in=left_in, right_in=right_in, site_blocks=site_blocks, sectors=sectors, site_operator=site_operator, sector_sizes=sector_sizes)


def sector_mask(sector_sizes, block_width):
    live = jnp.arange(block_width, dtype=jnp.int32)[None, :] < sector_sizes[:, None]
    return live[:, :, None] & live[:, None, :]


def finish(total, live_mask):
    return jnp.where(live_mask, total, 0.0).astype(jnp.bfloat16)


def scaled_blocks(blocks, weights):
    scaled = (blocks.astype(jnp.float32) * weights[:, None, None]).astype(jnp.bfloat16)
    return lax.optimization_barrier(scaled).astype(jnp.float32)


def left_terms(environ, blocks, source, target, weights, num_sectors):
    chosen = jnp.take(environ, source, axis=0).astype(jnp.float32)
    wide_blocks = blocks.astype(jnp.float32)
    scaled = scaled_blocks(blocks, weights)
    halfway = jnp.einsum('kab,kbc->kac', chosen, wide_blocks, precision=lax.Precision.HIGHEST)
    halfway = lax.optimization_barrier(halfway.astype(jnp.bfloat16)).astype(jnp.float32)
    mapped = jnp.einsum('kai,kac->kic', scaled, halfway, precision=lax.Precision.HIGHEST)
    onehot = (target[:, None] == jnp.arange(num_sectors, dtype=jnp.int32)[None, :]).astype(jnp.float32)
    return jnp.einsum('kt,kic->tic', onehot, mapped, precision=lax.Precision.HIGHEST)


def right_terms(environ, blocks, source, target, weights, num_sectors):
    chosen = jnp.take(environ, target, axis=0).astype(jnp.float32)
    wide_blocks = blocks.astype(jnp.float32)
    scaled = scaled_blocks(blocks, weights)
    halfway = jnp.einsum('kab,kbc->kac', wide_blocks, chosen, precision=lax.Precision.HIGHEST)
    halfway = lax.optimization_barrier(halfway.astype(jnp.bfloat16)).astype(jnp.float32)
    mapped = jnp.einsum('kac,kdc->kad', halfway, scaled, precision=lax.Precision.HIGHEST)
    onehot = (source[:, None] == jnp.arange(num_sectors, dtype=jnp.int32)[None, :]).astype(jnp.float32)
    return jnp.einsum('ks,kad->sad', onehot, mapped, precision=lax.Precision.HIGHEST)


def reference(left_in, right_in, site_blocks, sectors, site_operator, sector_sizes):
    live_mask = sector_mask(sector_sizes, B)
    pair_blocks = site_blocks.reshape(N_SEG, 2, NBLK, B, B)
    pair_sectors = sectors.reshape(N_SEG, 2, NBLK, 2)
    pair_ops = jnp.transpose(site_operator.reshape(N_SEG, 2, TERMS, NBLK), (0, 2, 1, 3))
    left_start = finish(left_in.astype(jnp.float32), live_mask)
    right_start = finish(right_in.astype(jnp.float32), live_mask)

    def segment_left(packed):
        environs, site_pair, sector_pair, term_ops = packed

        def one_term(environ, weights):
            inner = finish(left_terms(environ, site_pair[0], sector_pair[0, :, 0], sector_pair[0, :, 1], weights[0], NS), live_mask)
            return finish(left_terms(inner, site_pair[1], sector_pair[1, :, 0], sector_pair[1, :, 1], weights[1], NS), live_mask)

        return jax.vmap(one_term)(environs, term_ops)

    def segment_right(packed):
        environs, site_pair, sector_pair, term_ops = packed

        def one_term(environ, weights):
            inner = finish(right_terms(environ, site_pair[1], sector_pair[1, :, 0], sector_pair[1, :, 1], weights[1], NS), live_mask)
            return finish(right_terms(inner, site_pair[0], sector_pair[0, :, 0], sector_pair[0, :, 1], weights[0], NS), live_mask)

        return jax.vmap(one_term)(environs, term_ops)

    state_left = left_start
    state_right = right_start
    for sweep in range(STEPS):
        incoming_left = jnp.concatenate([left_start[:1], state_left[:-1]], axis=0)
        incoming_right = jnp.concatenate([state_right[1:], right_start[-1:]], axis=0)
        state_left = lax.map(segment_left, (incoming_left, pair_blocks, pair_sectors, pair_ops))
        state_right = lax.map(segment_right, (incoming_right, pair_blocks, pair_sectors, pair_ops))
    left_sum = jnp.sum(state_left.astype(jnp.float32), axis=1)
    right_sum = jnp.sum(state_right.astype(jnp.float32), axis=1)
    return state_left, state_right, left_sum, right_sum
```

```python
import jax
import jax.numpy as jnp
from jax import lax
from jax.experimental import pallas as pl
from jax.experimental.pallas import tpu as pltpu
from jax.sharding import PartitionSpec as P

F32 = jnp.float32
BF16 = jnp.bfloat16
VMEM = pl.BlockSpec(memory_space=pltpu.VMEM)
SMEM = pl.BlockSpec(memory_space=pltpu.SMEM)
ANY = pl.BlockSpec(memory_space=pl.ANY)
NY, NX = 4, 2
TERMS = NY * NX
PER_SECTOR = 4
NN = (((1,), (0,)), ((), ()))
TN = (((0,), (0,)), ((), ()))
NT = (((1,), (1,)), ((), ()))
OWN, DOWN, UP, OPP, X_OWN, X_DOWN, X_UP, X_OPP, FIRST_SEG, LAST_SEG = range(10)


def dot(a, b, dims):
    return lax.dot_general(a, b, dims, preferred_element_type=F32)


def op_route(dy, dx):
    return [(o, ((o // NX + dy) % NY) * NX + ((o % NX) ^ dx)) for o in range(TERMS)]


def hop(block, dy, dx):
    return lax.ppermute(block, "op", op_route(dy, dx))


def along_segments(block, distance):
    devices = range(lax.axis_size("seg"))
    route = [(i - distance, i) for i in devices if i - distance in devices]
    return lax.ppermute(block, "seg", route)


def live(sizes, sector, width):
    rows = lax.broadcasted_iota(jnp.int32, (width, width), 0)
    cols = lax.broadcasted_iota(jnp.int32, (width, width), 1)
    return jnp.maximum(rows, cols) < sizes[sector]


def finish(total, sizes, out, extra=None):
    num, width, _ = total.shape

    @pl.loop(0, num, step=4)
    def _(start):
        for t in range(4):
            kept = jnp.where(live(sizes, start + t, width), total[start + t], 0.0).astype(BF16)
            out[start + t] = kept
            if extra is not None:
                extra(start + t, kept)


def group(order, at, sector):
    return [order[at + PER_SECTOR * sector + j] for j in range(PER_SECTOR)]


def stage(count, unroll):
    def run(body):
        @pl.loop(0, count, step=unroll)
        def _(start):
            for u in range(unroll):
                body(start + u)

    return run


def sorted_left(env, blocks, half, total, order, weights, site, unroll):
    num, width, _ = total.shape
    n = num * PER_SECTOR

    @stage(num, unroll)
    def _(s):
        members = group(order, 2 * site * n, s)
        wide = jnp.concatenate([blocks[k] for k in members], axis=1)
        found = dot(env[s], wide, NN)
        for j, k in enumerate(members):
            piece = found[:, j * width : (j + 1) * width]
            half[k] = (piece * weights[site * n + k]).astype(BF16)

    @stage(num, unroll)
    def _(t):
        members = group(order, (2 * site + 1) * n, t)
        a = jnp.concatenate([blocks[k] for k in members], axis=0)
        y = jnp.concatenate([half[k] for k in members], axis=0)
        total[t] = dot(a, y, TN)


def sorted_right(env, blocks, half, total, order, weights, site, unroll):
    num, width, _ = total.shape
    n = num * PER_SECTOR

    @stage(num, unroll)
    def _(t):
        members = group(order, (2 * site + 1) * n, t)
        tall = jnp.concatenate([blocks[k] for k in members], axis=0)
        found = dot(tall, env[t], NN)
        for j, k in enumerate(members):
            piece = found[j * width : (j + 1) * width]
            half[k] = (piece * weights[site * n + k]).astype(BF16)

    @stage(num, unroll)
    def _(s):
        members = group(order, 2 * site * n, s)
        a = jnp.concatenate([blocks[k] for k in members], axis=1)
        z = jnp.concatenate([half[k] for k in members], axis=1)
        total[s] = dot(z, a, NT)


def add_left(env, total, blocks, sectors, weights, site, first, count, n):
    found = []
    for j in range(count):
        k = site * n + first + j
        block = blocks[j]
        half = (dot(env[sectors[2 * k]], block, NN) * weights[k]).astype(BF16)
        found.append((sectors[2 * k + 1], dot(block, half, TN)))
    for place, value in found:
        total[place] += value


def add_right(env, total, blocks, sectors, weights, site, first, count, n):
    found = []
    for j in range(count):
        k = site * n + first + j
        block = blocks[j]
        half = (dot(block, env[sectors[2 * k + 1]], NN) * weights[k]).astype(BF16)
        found.append((sectors[2 * k], dot(half, block, NT)))
    for place, value in found:
        total[place] += value


def call(body, outs, ins, scratch=(), flops=0):
    return pl.pallas_call(
        body,
        out_shape=[shape for _, shape in outs],
        in_specs=[spec for spec, _ in ins],
        out_specs=[spec for spec, _ in outs],
        scratch_shapes=list(scratch),
        compiler_params=pltpu.CompilerParams(vmem_limit_bytes=24 * 1024 * 1024),
        cost_estimate=pl.CostEstimate(flops=flops, bytes_accessed=6000000, transcendentals=0),
    )(*[array for _, array in ins])


def local(left_in, right_in, site_blocks, sectors, site_operator, sector_sizes):
    num, width = left_in.shape[2], left_in.shape[3]
    n = sectors.shape[1]
    share = n // TERMS
    per = num // TERMS
    env = jax.ShapeDtypeStruct((num, width, width), BF16)
    total = jax.ShapeDtypeStruct((num, width, width), F32)
    site_shape = jax.ShapeDtypeStruct((share, width, width), BF16)
    site_scratch = pltpu.VMEM((n, width, width), BF16)
    left_own, right_own = left_in[0, 0], right_in[0, 0]
    me = lax.axis_index("op")
    my_y, my_x = me // NX, me % NX
    seg = lax.axis_index("seg")
    shards = [((my_y + dy) % NY) * NX + (my_x ^ dx) for dx in (0, 1) for dy in (0, 3, 1, 2)]
    meta = jnp.stack(
        shards + [(seg == 0).astype(jnp.int32), (seg == lax.axis_size("seg") - 1).astype(jnp.int32)]
    )
    sec = sectors.reshape(-1)
    wts = site_operator.reshape(-1)

    own = site_blocks
    b_x = hop(own, 0, 1)
    down = hop(own, 1, 0)
    up = hop(own, -1, 0)
    left_arrived = along_segments(left_own, 1)
    right_arrived = along_segments(right_own, -1)
    x_down = hop(down, 0, 1)
    x_up = hop(b_x, -1, 0)
    opp = hop(down, 1, 0)

    def prepare(sec, sizes, meta, lo, la, ro, ra, le, re, order, count):
        @pl.loop(0, num)
        def _(t):
            alive = live(sizes, t, width)
            from_left = jnp.where(meta[FIRST_SEG] == 1, lo[t], la[t])
            from_right = jnp.where(meta[LAST_SEG] == 1, ro[t], ra[t])
            le[t] = jnp.where(alive, from_left.astype(F32), 0.0).astype(BF16)
            re[t] = jnp.where(alive, from_right.astype(F32), 0.0).astype(BF16)
            for table in range(4):
                count[table * num + t] = 0

        @pl.loop(0, n)
        def _(k):
            for table in range(4):
                site, side = table // 2, table % 2
                sector = sec[2 * (site * n + k) + side]
                seen = count[table * num + sector]
                order[table * n + PER_SECTOR * sector + seen] = k
                count[table * num + sector] = seen + 1

    le, re, order = call(
        prepare,
        [(VMEM, env), (VMEM, env), (SMEM, jax.ShapeDtypeStruct((4 * n,), jnp.int32))],
        [(SMEM, sec), (SMEM, sector_sizes), (SMEM, meta)]
        + [(VMEM, a) for a in (left_own, left_arrived, right_own, right_arrived)],
        scratch=[pltpu.SMEM((4 * num,), jnp.int32)],
    )

    def near(sec, wts, meta, le, re, own, down, up, b_x, lt, rt, token):
        @pl.loop(0, num, step=4)
        def _(t):
            for u in range(4):
                lt[t + u] = jnp.zeros((width, width), F32)
                rt[t + u] = jnp.zeros((width, width), F32)

        for ref, slot in ((own, OWN), (down, DOWN), (up, UP), (b_x, X_OWN)):
            first = meta[slot] * share
            add_left(le, lt, ref.at[0], sec, wts, 0, first, share, n)
            add_right(re, rt, ref.at[1], sec, wts, 1, first, share, n)
        token[0] = 0

    lt, rt, token = call(
        near,
        [(VMEM, total), (VMEM, total), (SMEM, jax.ShapeDtypeStruct((1,), jnp.int32))],
        [(SMEM, sec), (SMEM, wts), (SMEM, meta)]
        + [(VMEM, a) for a in (le, re, own, down, up, b_x)],
        flops=2 * 48 * 4 * 128**3,
    )

    def pick(token, x_down, x_up, out0, out1, sems):
        copies = [
            pltpu.make_async_copy(x_down.at[0], out0, sems.at[0]),
            pltpu.make_async_copy(x_up.at[1], out1, sems.at[1]),
        ]
        for copy in copies:
            copy.start()
        for copy in copies:
            copy.wait()

    send0, send1 = call(
        pick,
        [(ANY, site_shape), (ANY, site_shape)],
        [(SMEM, token), (ANY, x_down), (ANY, x_up)],
        scratch=[pltpu.SemaphoreType.DMA((2,))],
    )
    x_opp0 = hop(send0, 1, 0)
    x_opp1 = hop(send1, -1, 0)

    def further(sec, wts, meta, le, re, lt_in, rt_in, opp, x_down, x_up, lt, rt):
        @pl.loop(0, num, step=4)
        def _(t):
            for u in range(4):
                lt[t + u] = lt_in[t + u]
                rt[t + u] = rt_in[t + u]

        for ref, slot in ((x_down, X_DOWN), (x_up, X_UP), (opp, OPP)):
            first = meta[slot] * share
            add_left(le, lt, ref.at[0], sec, wts, 0, first, share, n)
            add_right(re, rt, ref.at[1], sec, wts, 1, first, share, n)

    lt, rt = call(
        further,
        [(VMEM, total), (VMEM, total)],
        [(SMEM, sec), (SMEM, wts), (SMEM, meta)]
        + [(VMEM, a) for a in (le, re, lt, rt, opp, x_down, x_up)],
        flops=2 * 36 * 4 * 128**3,
    )

    slots = (OWN, DOWN, UP, X_OWN, X_DOWN, X_UP, OPP)
    known = (own, down, up, b_x, x_down, x_up, opp)

    def last(sec, order, wts, sizes, meta, le, re, lt_in, rt_in, late0, late1, *rest):
        known, rest = rest[:7], rest[7:]
        left_out, right_out, both, lt, rt, le2, re2, done_left, done_right = rest[:9]
        blocks0, blocks1, half, sems, out_sems = rest[9:]
        copies = []
        for site, late, blocks in ((1, late1, blocks1), (0, late0, blocks0)):
            for i, slot in enumerate(slots + (X_OPP,)):
                source = late if slot == X_OPP else known[i].at[site]
                first = pl.multiple_of(meta[slot] * share, share)
                copies.append(
                    pltpu.make_async_copy(
                        source, blocks.at[pl.ds(first, share)], sems.at[site * TERMS + i]
                    )
                )
        for copy in copies:
            copy.start()

        @pl.loop(0, num, step=4)
        def _(t):
            for u in range(4):
                lt[t + u] = lt_in[t + u]
                rt[t + u] = rt_in[t + u]

        first = meta[X_OPP] * share
        add_left(le, lt, late0, sec, wts, 0, first, share, n)
        finish(lt, sizes, le2)
        add_right(re, rt, late1, sec, wts, 1, first, share, n)
        finish(rt, sizes, re2)
        for copy in copies[:TERMS]:
            copy.wait()
        sorted_left(le2, blocks1, half, lt, order, wts, 1, 12)

        def send_out(done, out, at):
            parts = [
                pltpu.make_async_copy(done, out, out_sems.at[2 * at]),
                pltpu.make_async_copy(
                    done.reshape(TERMS, per, width, width),
                    both.at[:, pl.ds(at * per, per)],
                    out_sems.at[2 * at + 1],
                ),
            ]
            for part in parts:
                part.start()
            return parts

        finish(lt, sizes, done_left)
        sent = send_out(done_left, left_out, 0)
        for copy in copies[TERMS:]:
            copy.wait()
        sorted_right(re2, blocks0, half, rt, order, wts, 0, 12)
        finish(rt, sizes, done_right)
        sent += send_out(done_right, right_out, 1)
        for part in sent:
            part.wait()

    packed = jax.ShapeDtypeStruct((TERMS, 2 * per, width, width), BF16)
    left_state, right_state, both = call(
        last,
        [(ANY, env), (ANY, env), (ANY, packed)],
        [(SMEM, sec), (SMEM, order), (SMEM, wts), (SMEM, sector_sizes), (SMEM, meta)]
        + [(VMEM, a) for a in (le, re, lt, rt, x_opp0, x_opp1)]
        + [(ANY, a) for a in known],
        scratch=[pltpu.VMEM(total.shape, F32)] * 2
        + [pltpu.VMEM(env.shape, BF16)] * 4
        + [site_scratch] * 3
        + [pltpu.SemaphoreType.DMA((2 * TERMS,)), pltpu.SemaphoreType.DMA((4,))],
        flops=2 * 204 * 2 * 128**3,
    )
    parts = lax.all_to_all(both, "op", 0, 0, tiled=True)

    def sum_terms(parts, left_sum, right_sum):
        for t in range(per):
            for out, at in ((left_sum, t), (right_sum, per + t)):
                value = parts[0, at].astype(F32)
                for term in range(1, TERMS):
                    value += parts[term, at].astype(F32)
                out[t] = value

    part = jax.ShapeDtypeStruct((per, width, width), F32)
    left_sum, right_sum = call(sum_terms, [(VMEM, part), (VMEM, part)], [(VMEM, parts)])
    return left_state[None, None], right_state[None, None], left_sum[None], right_sum[None]


def solution(mesh):
    placed = (
        P("seg", "op", None, None, None),
        P("seg", "op", None, None, None),
        P("seg", "op", None, None),
        P("seg", None, None),
        P("seg", "op", None),
        P(),
    )
    return jax.shard_map(
        local,
        mesh=mesh,
        in_specs=placed,
        out_specs=(
            P("seg", "op", None, None, None),
            P("seg", "op", None, None, None),
            P("seg", "op", None, None),
            P("seg", "op", None, None),
        ),
        check_vma=False,
    )
```

```python
import jax
import jax.numpy as jnp
from jax import lax
from jax.experimental import pallas as pl
from jax.experimental.pallas import tpu as pltpu
from jax.sharding import PartitionSpec as P

F32 = jnp.float32
BF16 = jnp.bfloat16
VMEM = pl.BlockSpec(memory_space=pltpu.VMEM)
SMEM = pl.BlockSpec(memory_space=pltpu.SMEM)
HBM = pl.BlockSpec(memory_space=pltpu.HBM)
NY, NX = 4, 2
TERMS = NY * NX
PER_SECTOR = 4
UNROLL = 12
NN = (((1,), (0,)), ((), ()))
TN = (((0,), (0,)), ((), ()))
NT = (((1,), (1,)), ((), ()))
OWN, DOWN, UP, OPP, X_OWN, X_DOWN, X_UP, X_OPP = range(8)
STEPS_OF = ((0, 0), (-1, 0), (1, 0), (2, 0), (0, 1), (-1, 1), (1, 1), (2, 1))


def dot(a, b, dims):
    return lax.dot_general(a, b, dims, preferred_element_type=F32)


def op_route(dy, dx):
    return [(o, ((o // NX + dy) % NY) * NX + ((o % NX) ^ dx)) for o in range(TERMS)]


def hop(block, dy, dx):
    return lax.ppermute(block, "op", op_route(dy, dx))


def along_segments(block, distance, across):
    size = lax.axis_size("seg")
    route = [(i - distance, i) for i in range(size) if i - distance in range(size)]
    middle = {size // 2 - 1, size // 2}
    route = [pair for pair in route if (set(pair) == middle) == across]
    return lax.ppermute(block, "seg", route)


def live(sizes, sector, width):
    rows = lax.broadcasted_iota(jnp.int32, (width, width), 0)
    cols = lax.broadcasted_iota(jnp.int32, (width, width), 1)
    return jnp.maximum(rows, cols) < sizes[sector]


def finish(total, sizes, out):
    num, width, _ = total.shape

    @pl.loop(0, num, step=4)
    def _(start):
        for u in range(4):
            alive = live(sizes, start + u, width)
            out[start + u] = jnp.where(alive, total[start + u].astype(F32), 0.0).astype(BF16)


def rank_blocks(sectors, out, n):
    place = lax.broadcasted_iota(jnp.int32, (n, n), 0)
    block = lax.broadcasted_iota(jnp.int32, (n, n), 1)
    earlier = jnp.where(place < block, 1.0, 0.0).astype(BF16)
    index = lax.broadcasted_iota(jnp.int32, (8, n), 1).astype(F32).astype(BF16)
    for site in range(2):
        for side in range(2):
            mine = sectors[site, side : side + 1, :] == place // PER_SECTOR
            seen = dot(jnp.where(mine, 1.0, 0.0).astype(BF16), earlier, NN)
            wanted = (place % PER_SECTOR).astype(F32)
            chosen = jnp.where(jnp.logical_and(mine, seen == wanted), 1.0, 0.0).astype(BF16)
            row = dot(index, chosen, NT)[:1].astype(jnp.int32)
            out[2 * site + side : 2 * site + side + 1, :n] = row


def group(order, table, sector):
    return [order[table, PER_SECTOR * sector + j] for j in range(PER_SECTOR)]


def stage(first, last, unroll, body):
    @pl.loop(first, last, step=unroll)
    def _(start):
        for u in range(unroll):
            body(start + u)


def keep(out, sizes=None):
    def emit(sector, value):
        if sizes is None:
            out[sector] = value
        else:
            alive = live(sizes, sector, value.shape[0])
            out[sector] = jnp.where(alive, value, 0.0).astype(BF16)

    return emit


def left_outward(env, blocks, half, order, weights, site, unroll):
    num, width, _ = env.shape

    def outward(s):
        members = group(order, 2 * site, s)
        found = dot(env[s], jnp.concatenate([blocks[k] for k in members], axis=1), NN)
        for j, k in enumerate(members):
            piece = found[:, j * width : (j + 1) * width]
            half[k] = (piece * weights[site, 0, k]).astype(BF16)

    stage(0, num, unroll, outward)


def left_inward(blocks, half, emit, order, site, num, unroll, cuts=(0,), done=None):
    def inward(t):
        members = group(order, 2 * site + 1, t)
        a = jnp.concatenate([blocks[k] for k in members], axis=0)
        y = jnp.concatenate([half[k] for k in members], axis=0)
        emit(t, dot(a, y, TN))

    in_parts(inward, num, unroll, cuts, done)


def right_outward(env, blocks, half, order, weights, site, unroll):
    num, width, _ = env.shape

    def outward(t):
        members = group(order, 2 * site + 1, t)
        found = dot(jnp.concatenate([blocks[k] for k in members], axis=0), env[t], NN)
        for j, k in enumerate(members):
            piece = found[j * width : (j + 1) * width]
            half[k] = (piece * weights[site, 0, k]).astype(BF16)

    stage(0, num, unroll, outward)


def right_inward(blocks, half, emit, order, site, num, unroll, cuts=(0,), done=None):
    def inward(s):
        members = group(order, 2 * site, s)
        a = jnp.concatenate([blocks[k] for k in members], axis=1)
        z = jnp.concatenate([half[k] for k in members], axis=1)
        emit(s, dot(z, a, NT))

    in_parts(inward, num, unroll, cuts, done)


def in_parts(body, num, unroll, cuts, done):
    for first, last in zip(cuts, tuple(cuts[1:]) + (num,)):
        stage(first, last, min(unroll, last - first), body)
        if done is not None:
            done(first, last)


def add_left(env, total, blocks, sectors, weights, site, first, count):
    found = []
    for j in range(count):
        k = first + j
        block = blocks[j]
        half = (dot(env[sectors[site, 0, k]], block, NN) * weights[site, 0, k]).astype(BF16)
        found.append((sectors[site, 1, k], dot(block, half, TN)))
    for place, value in found:
        total[place] += value


def add_right(env, total, blocks, sectors, weights, site, first, count):
    found = []
    for j in range(count):
        k = first + j
        block = blocks[j]
        half = (dot(block, env[sectors[site, 1, k]], NN) * weights[site, 0, k]).astype(BF16)
        found.append((sectors[site, 0, k], dot(half, block, NT)))
    for place, value in found:
        total[place] += value


def shard_at(slot):
    dy, dx = STEPS_OF[slot]
    me = lax.axis_index("op")
    return ((me // NX + dy + NY) % NY) * NX + ((me % NX) ^ dx)


def after(token, *arrays):
    def body(token, *refs):
        pass

    return pl.pallas_call(
        body,
        out_shape=[jax.ShapeDtypeStruct(a.shape, a.dtype) for a in arrays],
        in_specs=[SMEM] + [HBM] * len(arrays),
        out_specs=[HBM] * len(arrays),
        input_output_aliases={1 + i: i for i in range(len(arrays))},
    )(token, *arrays)


def call(body, outs, ins, scratch=(), flops=0, vmem=60, aliases={}):
    return pl.pallas_call(
        body,
        out_shape=[shape for _, shape in outs],
        in_specs=[spec for spec, _ in ins],
        out_specs=[spec for spec, _ in outs],
        scratch_shapes=list(scratch),
        input_output_aliases=aliases,
        compiler_params=pltpu.CompilerParams(vmem_limit_bytes=vmem * 1024 * 1024),
        cost_estimate=pl.CostEstimate(flops=flops, bytes_accessed=6000000, transcendentals=0),
    )(*[array for _, array in ins])


def local(left_in, right_in, site_blocks, sectors, site_operator, sector_sizes):
    num, width = left_in.shape[2], left_in.shape[3]
    n = sectors.shape[1]
    share = n // TERMS
    per = num // TERMS
    env = jax.ShapeDtypeStruct((num, width, width), BF16)
    total = jax.ShapeDtypeStruct((num, width, width), F32)
    site_shape = jax.ShapeDtypeStruct((share, width, width), BF16)
    token_shape = jax.ShapeDtypeStruct((1,), jnp.int32)
    env_scratch = pltpu.VMEM(env.shape, BF16)
    total_scratch = pltpu.VMEM(total.shape, F32)
    site_scratch = pltpu.VMEM((n, width, width), BF16)
    sec = jnp.transpose(sectors, (0, 2, 1))
    wts = site_operator

    def move(pairs, sems):
        copies = [
            pltpu.make_async_copy(source, into, sems.at[i])
            for i, (source, into) in enumerate(pairs)
        ]
        for copy in copies:
            copy.start()
        return copies

    def wait(copies):
        for copy in copies:
            copy.wait()

    own = site_blocks
    b_x = hop(own, 0, 1)
    down = hop(own, 1, 0)
    up = hop(own, -1, 0)

    def prepare(sizes, sec_rows, lo_in, ro_in, lo_out, ro_out, order, left, right, ranked, sems):
        coming = move([(lo_in, left), (ro_in, right)], sems.at[pl.ds(0, 2)])
        rank_blocks(sec_rows, ranked, n)
        ranking = move([(ranked, order)], sems.at[pl.ds(2, 1)])
        going = []
        for i, (env_ref, out) in enumerate(((left, lo_out), (right, ro_out))):
            coming[i].wait()
            finish(env_ref, sizes, env_ref)
            going += move([(env_ref, out)], sems.at[pl.ds(3 + i, 1)])
        wait(ranking + going)

    left_own, right_own, order = call(
        prepare,
        [(HBM, env)] * 2 + [(SMEM, jax.ShapeDtypeStruct((4, 128), jnp.int32))],
        [(SMEM, sector_sizes), (VMEM, sec), (HBM, left_in[0, 0]), (HBM, right_in[0, 0])],
        scratch=[env_scratch] * 2
        + [pltpu.VMEM((4, 128), jnp.int32), pltpu.SemaphoreType.DMA((5,))],
    )
    left_arrived = along_segments(left_own, 1, False)
    right_arrived = along_segments(right_own, -1, False)
    x_up = hop(b_x, -1, 0)
    x_down = hop(down, 0, 1)
    opp = hop(down, 1, 0)

    def seg_flags():
        seg, size = lax.axis_index("seg"), lax.axis_size("seg")
        return seg == 0, seg == size - 1

    def choose(pairs, into, sem):
        for flag, source in pairs:

            @pl.when(flag)
            def _():
                pltpu.make_async_copy(source, into, sem).start()

        return pltpu.make_async_copy(pairs[0][1], into, sem)

    pair_scratch = pltpu.VMEM((2, share, width, width), BF16)
    half_scratch = pltpu.VMEM((share, width, width), BF16)

    def near(wts, sec, lo, la, own, down, up, b_x, lt_out, token, left, lt, *rest):
        ins, sems, env_sem = rest[:4], rest[4], rest[5]
        first_seg, _ = seg_flags()
        edges = ((first_seg, lo), (jnp.logical_not(first_seg), la))
        coming_left = choose(edges, left, env_sem)
        coming = move([(a.at[0], b) for a, b in zip((own, down, up, b_x), ins)], sems)
        token[0] = 0

        @pl.loop(0, num, step=4)
        def _(t):
            for u in range(4):
                lt[t + u] = jnp.zeros((width, width), F32)

        coming_left.wait()
        for ref, slot, copy in zip(ins, (OWN, DOWN, UP, X_OWN), coming):
            copy.wait()
            add_left(left, lt, ref, sec, wts, 0, shard_at(slot) * share, share)
        wait(move([(lt, lt_out)], sems))

    lt, token = call(
        near,
        [(HBM, total), (SMEM, token_shape)],
        [(SMEM, wts), (SMEM, sec)]
        + [(HBM, a) for a in (left_own, left_arrived, own, down, up, b_x)],
        scratch=[env_scratch, total_scratch]
        + [half_scratch] * 4
        + [pltpu.SemaphoreType.DMA((4,)), pltpu.SemaphoreType.DMA(())],
        flops=2 * 48 * 2 * 128**3,
    )

    def pick(token, x_down, x_up, lo, ro, out0, out1, lo_out, ro_out, sems):
        wait(move([(x_down.at[0], out0), (x_up.at[1], out1)], sems))

    send0, send1, left_own, right_own = call(
        pick,
        [(VMEM, site_shape), (VMEM, site_shape), (HBM, env), (HBM, env)],
        [(SMEM, token)] + [(HBM, a) for a in (x_down, x_up, left_own, right_own)],
        scratch=[pltpu.SemaphoreType.DMA((2,))],
        vmem=4,
        aliases={3: 2, 4: 3},
    )
    x_opp0 = hop(send0, 1, 0)
    x_opp1 = hop(send1, -1, 0)
    left_across = along_segments(left_own, 1, True)
    right_across = along_segments(right_own, -1, True)

    def further(wts, sec, lo, la, lt_in, opp, x_down, x_up, lt_out, left, lt, *rest):
        ins, sems = rest[:3], rest[3]
        first_seg, _ = seg_flags()
        edges = ((first_seg, lo), (jnp.logical_not(first_seg), la))
        coming = [choose(edges, left, sems.at[0])] + move([(lt_in, lt)], sems.at[pl.ds(1, 1)])
        froms = [a.at[0] for a in (opp, x_down, x_up)]
        blocks = move(list(zip(froms, ins)), sems.at[pl.ds(2, 3)])
        wait(coming)
        for ref, slot, copy in zip(ins, (OPP, X_DOWN, X_UP), blocks):
            copy.wait()
            add_left(left, lt, ref, sec, wts, 0, shard_at(slot) * share, share)
        wait(move([(lt, lt_out)], sems.at[pl.ds(1, 1)]))

    (lt,) = call(
        further,
        [(HBM, total)],
        [(SMEM, wts), (SMEM, sec)] + [(HBM, a) for a in (left_own, left_arrived, lt, opp, x_down, x_up)],
        scratch=[env_scratch, total_scratch]
        + [half_scratch] * 3
        + [pltpu.SemaphoreType.DMA((5,))],
        flops=2 * 36 * 2 * 128**3,
    )

    slots = (OWN, X_OWN, DOWN, UP, OPP, X_DOWN, X_UP)
    pairs = (own, b_x, down, up, opp, x_down, x_up)

    def last(wts, sizes, sec, order, lo, la, lx, ro, ra, rx, lt_in, late0, late1, *rest):
        pairs, rest = rest[: TERMS - 1], rest[TERMS - 1 :]
        left_out, right_out, both, left, right, lt, done_left, done_right = rest[:8]
        blocks0, blocks1, half, sems, late_sems, out_sems = rest[8:]
        seg, middle = lax.axis_index("seg"), lax.axis_size("seg") // 2
        first_seg, last_seg = seg_flags()
        left_mid, right_mid = seg == middle, seg == middle - 1

        def places(site, blocks):
            refs = [pair.at[site] for pair in pairs]
            firsts = [pl.multiple_of(shard_at(slot) * share, share) for slot in slots]
            return [(ref, blocks.at[pl.ds(f, share)]) for ref, f in zip(refs, firsts)]

        first = shard_at(X_OPP) * share
        late = pl.ds(pl.multiple_of(first, share), share)
        for_left = move([(late0, blocks0.at[late]), (lt_in, lt)], late_sems)
        plain = jnp.logical_not(jnp.logical_or(first_seg, left_mid))
        edges = ((first_seg, lo), (left_mid, lx), (plain, la))
        for_left.append(choose(edges, left, late_sems.at[2]))
        copies1 = move([(late1, blocks1.at[late])], late_sems.at[pl.ds(3, 1)])
        plain = jnp.logical_not(jnp.logical_or(last_seg, right_mid))
        edges = ((last_seg, ro), (right_mid, rx), (plain, ra))
        copies1.append(choose(edges, right, late_sems.at[4]))
        copies1 += move(places(1, blocks1), sems.at[pl.ds(0, TERMS - 1)])
        wait(for_left)

        @pl.when(jnp.logical_not(left_mid))
        def _():
            add_left(left, lt, blocks0.at[late], sec, wts, 0, first, share)
            finish(lt, sizes, left)

        wait(copies1)
        copies0 = move(places(0, blocks0), sems.at[pl.ds(TERMS - 1, TERMS - 1)])

        right_outward(right, blocks1, half, order, wts, 1, UNROLL)
        right_inward(blocks1, half, keep(right, sizes), order, 1, num, UNROLL)
        wait(copies0)

        @pl.when(left_mid)
        def _():
            left_outward(left, blocks0, half, order, wts, 0, UNROLL)
            left_inward(blocks0, half, keep(left, sizes), order, 0, num, UNROLL)

        sent = []

        def sender(done, out, at):
            def send(begin, end):
                count = (end - begin) // per
                to = both.at[pl.ds(begin // per, count), pl.ds(at * per, per)]
                rows = pl.ds(begin, end - begin)
                packed = done.at[rows].reshape(count, per, width, width)
                going = [(done.at[rows], out.at[rows]), (packed, to)]
                sent.extend(move(going, out_sems.at[pl.ds(len(sent), 2)]))

            return send

        cuts = (0, num // 2)
        left_outward(left, blocks1, half, order, wts, 1, UNROLL)
        left_inward(
            blocks1, half, keep(done_left, sizes), order, 1, num, UNROLL,
            cuts, sender(done_left, left_out, 0),
        )
        right_outward(right, blocks0, half, order, wts, 0, UNROLL)
        right_inward(
            blocks0, half, keep(done_right, sizes), order, 0, num, UNROLL,
            cuts, sender(done_right, right_out, 1),
        )
        wait(sent)

    packed = jax.ShapeDtypeStruct((TERMS, 2 * per, width, width), BF16)
    left_state, right_state, both = call(
        last,
        [(HBM, env), (HBM, env), (HBM, packed)],
        [(SMEM, wts), (SMEM, sector_sizes), (SMEM, sec), (SMEM, order)]
        + [(HBM, a) for a in (left_own, left_arrived, left_across, right_own, right_arrived, right_across)]
        + [(HBM, a) for a in (lt, x_opp0, x_opp1)]
        + [(HBM, a) for a in pairs],
        scratch=[env_scratch] * 2
        + [total_scratch]
        + [env_scratch] * 2
        + [site_scratch] * 3
        + [pltpu.SemaphoreType.DMA((2 * TERMS - 2,))]
        + [pltpu.SemaphoreType.DMA((5,)), pltpu.SemaphoreType.DMA((8,))],
        flops=2 * 300 * 2 * 128**3,
    )
    parts = lax.all_to_all(both, "op", 0, 0, tiled=True)

    def sum_terms(parts, left_sum, right_sum):
        for t in range(per):
            for out, at in ((left_sum, t), (right_sum, per + t)):
                value = parts[0, at].astype(F32)
                for term in range(1, TERMS):
                    value += parts[term, at].astype(F32)
                out[t] = value

    part = jax.ShapeDtypeStruct((per, width, width), F32)
    left_sum, right_sum = call(sum_terms, [(VMEM, part), (VMEM, part)], [(VMEM, parts)], vmem=16)
    return left_state[None, None], right_state[None, None], left_sum[None], right_sum[None]


def solution(mesh):
    placed = (
        P("seg", "op", None, None, None),
        P("seg", "op", None, None, None),
        P("seg", "op", None, None),
        P("seg", None, None),
        P("seg", "op", None),
        P(),
    )
    return jax.shard_map(
        local,
        mesh=mesh,
        in_specs=placed,
        out_specs=(
            P("seg", "op", None, None, None),
            P("seg", "op", None, None, None),
            P("seg", "op", None, None),
            P("seg", "op", None, None),
        ),
        check_vma=False,
    )
```

```python
import jax
import jax.numpy as jnp
from jax import lax
from jax.experimental import pallas as pl
from jax.experimental.pallas import tpu as pltpu
from jax.sharding import PartitionSpec as P

F32 = jnp.float32
BF16 = jnp.bfloat16
VMEM = pl.BlockSpec(memory_space=pltpu.VMEM)
SMEM = pl.BlockSpec(memory_space=pltpu.SMEM)
HBM = pl.BlockSpec(memory_space=pltpu.HBM)
NY, NX = 4, 2
TERMS = NY * NX
PER_SECTOR = 4
UNROLL = 12
K_VMEM = 52
NN = (((1,), (0,)), ((), ()))
TN = (((0,), (0,)), ((), ()))
NT = (((1,), (1,)), ((), ()))
OWN, DOWN, UP, OPP, X_OWN, X_DOWN, X_UP, X_OPP = range(8)
STEPS_OF = ((0, 0), (-1, 0), (1, 0), (2, 0), (0, 1), (-1, 1), (1, 1), (2, 1))


def dot(a, b, dims):
    return lax.dot_general(a, b, dims, preferred_element_type=F32)


def op_route(dy, dx):
    return [(o, ((o // NX + dy) % NY) * NX + ((o % NX) ^ dx)) for o in range(TERMS)]


def hop(block, dy, dx):
    return lax.ppermute(block, "op", op_route(dy, dx))


def along_segments(block, distance):
    devices = range(lax.axis_size("seg"))
    route = [(i - distance, i) for i in devices if i - distance in devices]
    return lax.ppermute(block, "seg", route)


def live(sizes, sector, width):
    rows = lax.broadcasted_iota(jnp.int32, (width, width), 0)
    cols = lax.broadcasted_iota(jnp.int32, (width, width), 1)
    return jnp.maximum(rows, cols) < sizes[sector]


def finish(total, sizes, out):
    num, width, _ = total.shape

    @pl.loop(0, num, step=4)
    def _(start):
        for u in range(4):
            alive = live(sizes, start + u, width)
            out[start + u] = jnp.where(alive, total[start + u].astype(F32), 0.0).astype(BF16)


def rank_blocks(sectors, out, n):
    place = lax.broadcasted_iota(jnp.int32, (n, n), 0)
    block = lax.broadcasted_iota(jnp.int32, (n, n), 1)
    earlier = jnp.where(place < block, 1.0, 0.0).astype(BF16)
    index = lax.broadcasted_iota(jnp.int32, (8, n), 1).astype(F32).astype(BF16)
    for site in range(2):
        for side in range(2):
            mine = sectors[site, side : side + 1, :] == place // PER_SECTOR
            seen = dot(jnp.where(mine, 1.0, 0.0).astype(BF16), earlier, NN)
            wanted = (place % PER_SECTOR).astype(F32)
            chosen = jnp.where(jnp.logical_and(mine, seen == wanted), 1.0, 0.0).astype(BF16)
            row = dot(index, chosen, NT)[:1].astype(jnp.int32)
            out[2 * site + side : 2 * site + side + 1, :n] = row


def group(order, table, sector):
    return [order[table, PER_SECTOR * sector + j] for j in range(PER_SECTOR)]


def stage(first, last, unroll, body):
    @pl.loop(first, last, step=unroll)
    def _(start):
        for u in range(unroll):
            body(start + u)


def keep(out, sizes=None):
    def emit(sector, value):
        if sizes is None:
            out[sector] = value
        else:
            alive = live(sizes, sector, value.shape[0])
            out[sector] = jnp.where(alive, value, 0.0).astype(BF16)

    return emit


def left_outward(env, blocks, half, order, weights, site, unroll):
    num, width, _ = env.shape

    def outward(s):
        members = group(order, 2 * site, s)
        found = dot(env[s], jnp.concatenate([blocks[k] for k in members], axis=1), NN)
        for j, k in enumerate(members):
            piece = found[:, j * width : (j + 1) * width]
            half[k] = (piece * weights[site, 0, k]).astype(BF16)

    stage(0, num, unroll, outward)


def left_inward(blocks, half, emit, order, site, num, unroll, cuts=(0,), done=None):
    def inward(t):
        members = group(order, 2 * site + 1, t)
        a = jnp.concatenate([blocks[k] for k in members], axis=0)
        y = jnp.concatenate([half[k] for k in members], axis=0)
        emit(t, dot(a, y, TN))

    in_parts(inward, num, unroll, cuts, done)


def right_outward(env, blocks, half, order, weights, site, unroll):
    num, width, _ = env.shape

    def outward(t):
        members = group(order, 2 * site + 1, t)
        found = dot(jnp.concatenate([blocks[k] for k in members], axis=0), env[t], NN)
        for j, k in enumerate(members):
            piece = found[j * width : (j + 1) * width]
            half[k] = (piece * weights[site, 0, k]).astype(BF16)

    stage(0, num, unroll, outward)


def right_inward(blocks, half, emit, order, site, num, unroll, cuts=(0,), done=None):
    def inward(s):
        members = group(order, 2 * site, s)
        a = jnp.concatenate([blocks[k] for k in members], axis=1)
        z = jnp.concatenate([half[k] for k in members], axis=1)
        emit(s, dot(z, a, NT))

    in_parts(inward, num, unroll, cuts, done)


def in_parts(body, num, unroll, cuts, done):
    for first, last in zip(cuts, tuple(cuts[1:]) + (num,)):
        stage(first, last, min(unroll, last - first), body)
        if done is not None:
            done(first, last)


def add_left(env, total, blocks, sectors, weights, site, first, count):
    found = []
    for j in range(count):
        k = first + j
        block = blocks[j]
        half = (dot(env[sectors[site, 0, k]], block, NN) * weights[site, 0, k]).astype(BF16)
        found.append((sectors[site, 1, k], dot(block, half, TN)))
    for place, value in found:
        total[place] += value


def add_right(env, total, blocks, sectors, weights, site, first, count):
    found = []
    for j in range(count):
        k = first + j
        block = blocks[j]
        half = (dot(block, env[sectors[site, 1, k]], NN) * weights[site, 0, k]).astype(BF16)
        found.append((sectors[site, 0, k], dot(half, block, NT)))
    for place, value in found:
        total[place] += value


def shard_at(slot):
    dy, dx = STEPS_OF[slot]
    me = lax.axis_index("op")
    return ((me // NX + dy + NY) % NY) * NX + ((me % NX) ^ dx)


def after(token, *arrays):
    def body(token, *refs):
        pass

    return pl.pallas_call(
        body,
        out_shape=[jax.ShapeDtypeStruct(a.shape, a.dtype) for a in arrays],
        in_specs=[SMEM] + [HBM] * len(arrays),
        out_specs=[HBM] * len(arrays),
        input_output_aliases={1 + i: i for i in range(len(arrays))},
    )(token, *arrays)


def call(body, outs, ins, scratch=(), flops=0, vmem=52):
    return pl.pallas_call(
        body,
        out_shape=[shape for _, shape in outs],
        in_specs=[spec for spec, _ in ins],
        out_specs=[spec for spec, _ in outs],
        scratch_shapes=list(scratch),
        compiler_params=pltpu.CompilerParams(vmem_limit_bytes=vmem * 1024 * 1024),
        cost_estimate=pl.CostEstimate(flops=flops, bytes_accessed=6000000, transcendentals=0),
    )(*[array for _, array in ins])


def local(left_in, right_in, site_blocks, sectors, site_operator, sector_sizes):
    num, width = left_in.shape[2], left_in.shape[3]
    n = sectors.shape[1]
    share = n // TERMS
    per = num // TERMS
    env = jax.ShapeDtypeStruct((num, width, width), BF16)
    total = jax.ShapeDtypeStruct((num, width, width), F32)
    site_shape = jax.ShapeDtypeStruct((share, width, width), BF16)
    token_shape = jax.ShapeDtypeStruct((1,), jnp.int32)
    env_scratch = pltpu.VMEM(env.shape, BF16)
    total_scratch = pltpu.VMEM(total.shape, F32)
    site_scratch = pltpu.VMEM((n, width, width), BF16)
    sec = jnp.transpose(sectors, (0, 2, 1))
    wts = site_operator

    def move(pairs, sems):
        copies = [
            pltpu.make_async_copy(source, into, sems.at[i])
            for i, (source, into) in enumerate(pairs)
        ]
        for copy in copies:
            copy.start()
        return copies

    def wait(copies):
        for copy in copies:
            copy.wait()

    own = site_blocks
    b_x = hop(own, 0, 1)
    down = hop(own, 1, 0)
    up = hop(own, -1, 0)

    def prepare(sizes, sec_rows, lo_in, ro_in, lo_out, ro_out, order, left, right, ranked, sems):
        coming = move([(lo_in, left), (ro_in, right)], sems.at[pl.ds(0, 2)])
        rank_blocks(sec_rows, ranked, n)
        ranking = move([(ranked, order)], sems.at[pl.ds(2, 1)])
        going = []
        for i, (env_ref, out) in enumerate(((left, lo_out), (right, ro_out))):
            coming[i].wait()
            finish(env_ref, sizes, env_ref)
            going += move([(env_ref, out)], sems.at[pl.ds(3 + i, 1)])
        wait(ranking + going)

    left_own, right_own, order = call(
        prepare,
        [(HBM, env)] * 2 + [(SMEM, jax.ShapeDtypeStruct((4, 128), jnp.int32))],
        [(SMEM, sector_sizes), (VMEM, sec), (HBM, left_in[0, 0]), (HBM, right_in[0, 0])],
        scratch=[env_scratch] * 2
        + [pltpu.VMEM((4, 128), jnp.int32), pltpu.SemaphoreType.DMA((5,))],
    )
    left_arrived = along_segments(left_own, 1)
    right_arrived = along_segments(right_own, -1)
    x_up = hop(b_x, -1, 0)
    x_down = hop(down, 0, 1)
    opp = hop(down, 1, 0)

    def seg_flags():
        seg, size = lax.axis_index("seg"), lax.axis_size("seg")
        return seg == 0, seg == size - 1

    def choose(pairs, into, sem):
        for flag, source in pairs:

            @pl.when(flag)
            def _():
                pltpu.make_async_copy(source, into, sem).start()

        return pltpu.make_async_copy(pairs[0][1], into, sem)

    pair_scratch = pltpu.VMEM((2, share, width, width), BF16)
    half_scratch = pltpu.VMEM((share, width, width), BF16)

    def near(wts, sec, lo, la, ra, own, down, up, b_x, lt_out, token, left, lt, *rest):
        ins, sems, env_sem = rest[:4], rest[4], rest[5]
        first_seg, _ = seg_flags()
        edges = ((first_seg, lo), (jnp.logical_not(first_seg), la))
        coming_left = choose(edges, left, env_sem)
        coming = move([(a.at[0], b) for a, b in zip((own, down, up, b_x), ins)], sems)
        token[0] = 0

        @pl.loop(0, num, step=4)
        def _(t):
            for u in range(4):
                lt[t + u] = jnp.zeros((width, width), F32)

        coming_left.wait()
        for ref, slot, copy in zip(ins, (OWN, DOWN, UP, X_OWN), coming):
            copy.wait()
            add_left(left, lt, ref, sec, wts, 0, shard_at(slot) * share, share)
        wait(move([(lt, lt_out)], sems))

    lt, token = call(
        near,
        [(HBM, total), (SMEM, token_shape)],
        [(SMEM, wts), (SMEM, sec)]
        + [(HBM, a) for a in (left_own, left_arrived, right_arrived, own, down, up, b_x)],
        scratch=[env_scratch, total_scratch]
        + [half_scratch] * 4
        + [pltpu.SemaphoreType.DMA((4,)), pltpu.SemaphoreType.DMA(())],
        flops=2 * 48 * 2 * 128**3,
    )

    def pick(token, x_down, x_up, out0, out1, sems):
        wait(move([(x_down.at[0], out0), (x_up.at[1], out1)], sems))

    send0, send1 = call(
        pick,
        [(VMEM, site_shape), (VMEM, site_shape)],
        [(SMEM, token), (HBM, x_down), (HBM, x_up)],
        scratch=[pltpu.SemaphoreType.DMA((2,))],
        vmem=4,
    )
    x_opp0 = hop(send0, 1, 0)
    x_opp1 = hop(send1, -1, 0)

    def further(wts, sec, lo, la, lt_in, opp, x_down, x_up, lt_out, left, lt, *rest):
        ins, sems = rest[:3], rest[3]
        first_seg, _ = seg_flags()
        edges = ((first_seg, lo), (jnp.logical_not(first_seg), la))
        coming = [choose(edges, left, sems.at[0])] + move([(lt_in, lt)], sems.at[pl.ds(1, 1)])
        froms = [a.at[0] for a in (opp, x_down, x_up)]
        blocks = move(list(zip(froms, ins)), sems.at[pl.ds(2, 3)])
        wait(coming)
        for ref, slot, copy in zip(ins, (OPP, X_DOWN, X_UP), blocks):
            copy.wait()
            add_left(left, lt, ref, sec, wts, 0, shard_at(slot) * share, share)
        wait(move([(lt, lt_out)], sems.at[pl.ds(1, 1)]))

    (lt,) = call(
        further,
        [(HBM, total)],
        [(SMEM, wts), (SMEM, sec)] + [(HBM, a) for a in (left_own, left_arrived, lt, opp, x_down, x_up)],
        scratch=[env_scratch, total_scratch]
        + [half_scratch] * 3
        + [pltpu.SemaphoreType.DMA((5,))],
        flops=2 * 36 * 2 * 128**3,
    )

    slots = (OWN, X_OWN, DOWN, UP, OPP, X_DOWN, X_UP)
    pairs = (own, b_x, down, up, opp, x_down, x_up)

    def last(wts, sizes, sec, order, lo, la, ro, ra, lt_in, late0, late1, *rest):
        pairs, rest = rest[: TERMS - 1], rest[TERMS - 1 :]
        left_out, right_out, both, left, right, lt, done_left, done_right = rest[:8]
        blocks0, blocks1, half, sems, late_sems, out_sems = rest[8:]
        first_seg, last_seg = seg_flags()

        def places(site, blocks):
            refs = [pair.at[site] for pair in pairs]
            firsts = [pl.multiple_of(shard_at(slot) * share, share) for slot in slots]
            return [(ref, blocks.at[pl.ds(f, share)]) for ref, f in zip(refs, firsts)]

        first = shard_at(X_OPP) * share
        late = pl.ds(pl.multiple_of(first, share), share)
        edges = ((first_seg, lo), (jnp.logical_not(first_seg), la))
        for_left = [choose(edges, left, late_sems.at[0])]
        for_left += move([(late0, blocks0.at[late]), (lt_in, lt)], late_sems.at[pl.ds(1, 2)])
        edges = ((last_seg, ro), (jnp.logical_not(last_seg), ra))
        copies1 = [choose(edges, right, late_sems.at[3])]
        copies1 += move([(late1, blocks1.at[late])], late_sems.at[pl.ds(4, 1)])
        copies1 += move(places(1, blocks1), sems.at[pl.ds(0, TERMS - 1)])
        wait(for_left)
        add_left(left, lt, blocks0.at[late], sec, wts, 0, first, share)
        finish(lt, sizes, left)
        wait(copies1)
        copies0 = move(places(0, blocks0), sems.at[pl.ds(TERMS - 1, TERMS - 1)])
        sent = []

        def sender(done, out, at):
            def send(begin, end):
                count = (end - begin) // per
                to = both.at[pl.ds(begin // per, count), pl.ds(at * per, per)]
                rows = pl.ds(begin, end - begin)
                packed = done.at[rows].reshape(count, per, width, width)
                going = [(done.at[rows], out.at[rows]), (packed, to)]
                sent.extend(move(going, out_sems.at[pl.ds(len(sent), 2)]))

            return send

        cuts = (0, num // 2)
        left_outward(left, blocks1, half, order, wts, 1, UNROLL)
        left_inward(
            blocks1, half, keep(done_left, sizes), order, 1, num, UNROLL,
            cuts, sender(done_left, left_out, 0),
        )
        right_outward(right, blocks1, half, order, wts, 1, UNROLL)
        right_inward(blocks1, half, keep(right, sizes), order, 1, num, UNROLL)
        wait(copies0)
        right_outward(right, blocks0, half, order, wts, 0, UNROLL)
        right_inward(
            blocks0, half, keep(done_right, sizes), order, 0, num, UNROLL,
            cuts, sender(done_right, right_out, 1),
        )
        wait(sent)

    packed = jax.ShapeDtypeStruct((TERMS, 2 * per, width, width), BF16)
    left_state, right_state, both = call(
        last,
        [(HBM, env), (HBM, env), (HBM, packed)],
        [(SMEM, wts), (SMEM, sector_sizes), (SMEM, sec), (SMEM, order)]
        + [(HBM, a) for a in (left_own, left_arrived, right_own, right_arrived)]
        + [(HBM, a) for a in (lt, x_opp0, x_opp1)]
        + [(HBM, a) for a in pairs],
        scratch=[env_scratch] * 2
        + [total_scratch]
        + [env_scratch] * 2
        + [site_scratch] * 3
        + [pltpu.SemaphoreType.DMA((2 * TERMS - 2,))]
        + [pltpu.SemaphoreType.DMA((5,)), pltpu.SemaphoreType.DMA((8,))],
        flops=2 * 300 * 2 * 128**3,
        vmem=K_VMEM,
    )
    parts = lax.all_to_all(both, "op", 0, 0, tiled=True)

    def sum_terms(parts, left_sum, right_sum):
        for t in range(per):
            for out, at in ((left_sum, t), (right_sum, per + t)):
                value = parts[0, at].astype(F32)
                for term in range(1, TERMS):
                    value += parts[term, at].astype(F32)
                out[t] = value

    part = jax.ShapeDtypeStruct((per, width, width), F32)
    left_sum, right_sum = call(sum_terms, [(VMEM, part), (VMEM, part)], [(VMEM, parts)], vmem=16)
    return left_state[None, None], right_state[None, None], left_sum[None], right_sum[None]


def solution(mesh):
    placed = (
        P("seg", "op", None, None, None),
        P("seg", "op", None, None, None),
        P("seg", "op", None, None),
        P("seg", None, None),
        P("seg", "op", None),
        P(),
    )
    return jax.shard_map(
        local,
        mesh=mesh,
        in_specs=placed,
        out_specs=(
            P("seg", "op", None, None, None),
            P("seg", "op", None, None, None),
            P("seg", "op", None, None),
            P("seg", "op", None, None),
        ),
        check_vma=False,
    )
```

```python
import jax
import jax.numpy as jnp
from jax import lax
from jax.experimental import pallas as pl
from jax.experimental.pallas import tpu as pltpu
from jax.sharding import PartitionSpec as P

F32 = jnp.float32
BF16 = jnp.bfloat16
VMEM = pl.BlockSpec(memory_space=pltpu.VMEM)
SMEM = pl.BlockSpec(memory_space=pltpu.SMEM)
HBM = pl.BlockSpec(memory_space=pltpu.HBM)
NY, NX = 4, 2
TERMS = NY * NX
PER_SECTOR = 4
UNROLL = 12
K_VMEM = 52
NN = (((1,), (0,)), ((), ()))
TN = (((0,), (0,)), ((), ()))
NT = (((1,), (1,)), ((), ()))
OWN, DOWN, UP, OPP, X_OWN, X_DOWN, X_UP, X_OPP = range(8)
STEPS_OF = ((0, 0), (-1, 0), (1, 0), (2, 0), (0, 1), (-1, 1), (1, 1), (2, 1))


def dot(a, b, dims):
    return lax.dot_general(a, b, dims, preferred_element_type=F32)


def op_route(dy, dx):
    return [(o, ((o // NX + dy) % NY) * NX + ((o % NX) ^ dx)) for o in range(TERMS)]


def hop(block, dy, dx):
    return lax.ppermute(block, "op", op_route(dy, dx))


def along_segments(block, step):
    size = lax.axis_size("seg")
    middle, end = (size // 2 - 1, 0) if step > 0 else (size // 2, size - 1)
    route = [(i, i + step) for i in range(size) if i != middle and 0 <= i + step < size]
    return lax.ppermute(block, "seg", route + [(middle, end)])


def from_end(block, step):
    size = lax.axis_size("seg")
    route = [(0, size // 2)] if step > 0 else [(size - 1, size // 2 - 1)]
    return lax.ppermute(block, "seg", route)


def live(sizes, sector, width):
    rows = lax.broadcasted_iota(jnp.int32, (width, width), 0)
    cols = lax.broadcasted_iota(jnp.int32, (width, width), 1)
    return jnp.maximum(rows, cols) < sizes[sector]


def finish(total, sizes, out):
    num, width, _ = total.shape

    @pl.loop(0, num, step=4)
    def _(start):
        for u in range(4):
            alive = live(sizes, start + u, width)
            out[start + u] = jnp.where(alive, total[start + u].astype(F32), 0.0).astype(BF16)


def rank_blocks(sectors, out, n):
    place = lax.broadcasted_iota(jnp.int32, (n, n), 0)
    block = lax.broadcasted_iota(jnp.int32, (n, n), 1)
    earlier = jnp.where(place < block, 1.0, 0.0).astype(BF16)
    index = lax.broadcasted_iota(jnp.int32, (8, n), 1).astype(F32).astype(BF16)
    for site in range(2):
        for side in range(2):
            mine = sectors[site, side : side + 1, :] == place // PER_SECTOR
            seen = dot(jnp.where(mine, 1.0, 0.0).astype(BF16), earlier, NN)
            wanted = (place % PER_SECTOR).astype(F32)
            chosen = jnp.where(jnp.logical_and(mine, seen == wanted), 1.0, 0.0).astype(BF16)
            row = dot(index, chosen, NT)[:1].astype(jnp.int32)
            out[2 * site + side : 2 * site + side + 1, :n] = row


def group(order, table, sector):
    return [order[table, PER_SECTOR * sector + j] for j in range(PER_SECTOR)]


def stage(first, last, unroll, body):
    @pl.loop(first, last, step=unroll)
    def _(start):
        for u in range(unroll):
            body(start + u)


def keep(out, sizes=None):
    def emit(sector, value):
        if sizes is None:
            out[sector] = value
        else:
            alive = live(sizes, sector, value.shape[0])
            out[sector] = jnp.where(alive, value, 0.0).astype(BF16)

    return emit


def left_outward(env, blocks, half, order, weights, site, unroll):
    num, width, _ = env.shape

    def outward(s):
        members = group(order, 2 * site, s)
        found = dot(env[s], jnp.concatenate([blocks[k] for k in members], axis=1), NN)
        for j, k in enumerate(members):
            piece = found[:, j * width : (j + 1) * width]
            half[k] = (piece * weights[site, 0, k]).astype(BF16)

    stage(0, num, unroll, outward)


def left_inward(blocks, half, emit, order, site, num, unroll, cuts=(0,), done=None):
    def inward(t):
        members = group(order, 2 * site + 1, t)
        a = jnp.concatenate([blocks[k] for k in members], axis=0)
        y = jnp.concatenate([half[k] for k in members], axis=0)
        emit(t, dot(a, y, TN))

    in_parts(inward, num, unroll, cuts, done)


def right_outward(env, blocks, half, order, weights, site, unroll):
    num, width, _ = env.shape

    def outward(t):
        members = group(order, 2 * site + 1, t)
        found = dot(jnp.concatenate([blocks[k] for k in members], axis=0), env[t], NN)
        for j, k in enumerate(members):
            piece = found[j * width : (j + 1) * width]
            half[k] = (piece * weights[site, 0, k]).astype(BF16)

    stage(0, num, unroll, outward)


def right_inward(blocks, half, emit, order, site, num, unroll, cuts=(0,), done=None):
    def inward(s):
        members = group(order, 2 * site, s)
        a = jnp.concatenate([blocks[k] for k in members], axis=1)
        z = jnp.concatenate([half[k] for k in members], axis=1)
        emit(s, dot(z, a, NT))

    in_parts(inward, num, unroll, cuts, done)


def in_parts(body, num, unroll, cuts, done):
    for first, last in zip(cuts, tuple(cuts[1:]) + (num,)):
        stage(first, last, min(unroll, last - first), body)
        if done is not None:
            done(first, last)


def add_left(env, total, blocks, sectors, weights, site, first, count):
    found = []
    for j in range(count):
        k = first + j
        block = blocks[j]
        half = (dot(env[sectors[site, 0, k]], block, NN) * weights[site, 0, k]).astype(BF16)
        found.append((sectors[site, 1, k], dot(block, half, TN)))
    for place, value in found:
        total[place] += value


def add_right(env, total, blocks, sectors, weights, site, first, count):
    found = []
    for j in range(count):
        k = first + j
        block = blocks[j]
        half = (dot(block, env[sectors[site, 1, k]], NN) * weights[site, 0, k]).astype(BF16)
        found.append((sectors[site, 0, k], dot(half, block, NT)))
    for place, value in found:
        total[place] += value


def shard_at(slot):
    dy, dx = STEPS_OF[slot]
    me = lax.axis_index("op")
    return ((me // NX + dy + NY) % NY) * NX + ((me % NX) ^ dx)


def after(token, *arrays):
    def body(token, *refs):
        pass

    return pl.pallas_call(
        body,
        out_shape=[jax.ShapeDtypeStruct(a.shape, a.dtype) for a in arrays],
        in_specs=[SMEM] + [HBM] * len(arrays),
        out_specs=[HBM] * len(arrays),
        input_output_aliases={1 + i: i for i in range(len(arrays))},
    )(token, *arrays)


def call(body, outs, ins, scratch=(), flops=0, vmem=52, aliases={}):
    return pl.pallas_call(
        body,
        out_shape=[shape for _, shape in outs],
        in_specs=[spec for spec, _ in ins],
        out_specs=[spec for spec, _ in outs],
        scratch_shapes=list(scratch),
        input_output_aliases=aliases,
        compiler_params=pltpu.CompilerParams(vmem_limit_bytes=vmem * 1024 * 1024),
        cost_estimate=pl.CostEstimate(flops=flops, bytes_accessed=6000000, transcendentals=0),
    )(*[array for _, array in ins])


def local(left_in, right_in, site_blocks, sectors, site_operator, sector_sizes):
    num, width = left_in.shape[2], left_in.shape[3]
    n = sectors.shape[1]
    share = n // TERMS
    per = num // TERMS
    env = jax.ShapeDtypeStruct((num, width, width), BF16)
    total = jax.ShapeDtypeStruct((num, width, width), F32)
    site_shape = jax.ShapeDtypeStruct((share, width, width), BF16)
    token_shape = jax.ShapeDtypeStruct((1,), jnp.int32)
    env_scratch = pltpu.VMEM(env.shape, BF16)
    total_scratch = pltpu.VMEM(total.shape, F32)
    site_scratch = pltpu.VMEM((n, width, width), BF16)
    sec = jnp.transpose(sectors, (0, 2, 1))
    wts = site_operator

    def move(pairs, sems):
        copies = [
            pltpu.make_async_copy(source, into, sems.at[i])
            for i, (source, into) in enumerate(pairs)
        ]
        for copy in copies:
            copy.start()
        return copies

    def wait(copies):
        for copy in copies:
            copy.wait()

    own = site_blocks
    b_x = hop(own, 0, 1)
    down = hop(own, 1, 0)
    up = hop(own, -1, 0)

    def prepare(sizes, sec_rows, lo_in, ro_in, lo_out, ro_out, order, left, right, ranked, sems):
        coming = move([(lo_in, left), (ro_in, right)], sems.at[pl.ds(0, 2)])
        rank_blocks(sec_rows, ranked, n)
        ranking = move([(ranked, order)], sems.at[pl.ds(2, 1)])
        going = []
        for i, (env_ref, out) in enumerate(((left, lo_out), (right, ro_out))):
            coming[i].wait()
            finish(env_ref, sizes, env_ref)
            going += move([(env_ref, out)], sems.at[pl.ds(3 + i, 1)])
        wait(ranking + going)

    left_own, right_own, order = call(
        prepare,
        [(HBM, env)] * 2 + [(SMEM, jax.ShapeDtypeStruct((4, 128), jnp.int32))],
        [(SMEM, sector_sizes), (VMEM, sec), (HBM, left_in[0, 0]), (HBM, right_in[0, 0])],
        scratch=[env_scratch] * 2
        + [pltpu.VMEM((4, 128), jnp.int32), pltpu.SemaphoreType.DMA((5,))],
    )
    left_arrived = along_segments(left_own, 1)
    right_arrived = along_segments(right_own, -1)
    x_up = hop(b_x, -1, 0)
    x_down = hop(down, 0, 1)
    opp = hop(down, 1, 0)

    def seg_flags():
        seg, size = lax.axis_index("seg"), lax.axis_size("seg")
        return seg == 0, seg == size - 1

    def choose(pairs, into, sem):
        for flag, source in pairs:

            @pl.when(flag)
            def _():
                pltpu.make_async_copy(source, into, sem).start()

        return pltpu.make_async_copy(pairs[0][1], into, sem)

    pair_scratch = pltpu.VMEM((2, share, width, width), BF16)
    half_scratch = pltpu.VMEM((share, width, width), BF16)

    def near(wts, sec, lo, la, ra, own, down, up, b_x, lt_out, token, left, lt, *rest):
        ins, sems, env_sem = rest[:4], rest[4], rest[5]
        first_seg, _ = seg_flags()
        edges = ((first_seg, lo), (jnp.logical_not(first_seg), la))
        coming_left = choose(edges, left, env_sem)
        coming = move([(a.at[0], b) for a, b in zip((own, down, up, b_x), ins)], sems)
        token[0] = 0

        @pl.loop(0, num, step=4)
        def _(t):
            for u in range(4):
                lt[t + u] = jnp.zeros((width, width), F32)

        coming_left.wait()
        for ref, slot, copy in zip(ins, (OWN, DOWN, UP, X_OWN), coming):
            copy.wait()
            add_left(left, lt, ref, sec, wts, 0, shard_at(slot) * share, share)
        wait(move([(lt, lt_out)], sems))

    lt, token = call(
        near,
        [(HBM, total), (SMEM, token_shape)],
        [(SMEM, wts), (SMEM, sec)]
        + [(HBM, a) for a in (left_own, left_arrived, right_arrived, own, down, up, b_x)],
        scratch=[env_scratch, total_scratch]
        + [half_scratch] * 4
        + [pltpu.SemaphoreType.DMA((4,)), pltpu.SemaphoreType.DMA(())],
        flops=2 * 48 * 2 * 128**3,
    )

    def pick(token, x_down, x_up, la, ra, out0, out1, la_out, ra_out, sems):
        wait(move([(x_down.at[0], out0), (x_up.at[1], out1)], sems))

    send0, send1, left_arrived, right_arrived = call(
        pick,
        [(VMEM, site_shape), (VMEM, site_shape), (HBM, env), (HBM, env)],
        [(SMEM, token)] + [(HBM, a) for a in (x_down, x_up, left_arrived, right_arrived)],
        scratch=[pltpu.SemaphoreType.DMA((2,))],
        vmem=4,
        aliases={3: 2, 4: 3},
    )
    left_middle = from_end(left_arrived, 1)
    right_middle = from_end(right_arrived, -1)
    x_opp0 = hop(send0, 1, 0)
    x_opp1 = hop(send1, -1, 0)

    def further(wts, sec, lo, la, lt_in, opp, x_down, x_up, lt_out, left, lt, *rest):
        ins, sems = rest[:3], rest[3]
        first_seg, _ = seg_flags()
        edges = ((first_seg, lo), (jnp.logical_not(first_seg), la))
        coming = [choose(edges, left, sems.at[0])] + move([(lt_in, lt)], sems.at[pl.ds(1, 1)])
        froms = [a.at[0] for a in (opp, x_down, x_up)]
        blocks = move(list(zip(froms, ins)), sems.at[pl.ds(2, 3)])
        wait(coming)
        for ref, slot, copy in zip(ins, (OPP, X_DOWN, X_UP), blocks):
            copy.wait()
            add_left(left, lt, ref, sec, wts, 0, shard_at(slot) * share, share)
        wait(move([(lt, lt_out)], sems.at[pl.ds(1, 1)]))

    (lt,) = call(
        further,
        [(HBM, total)],
        [(SMEM, wts), (SMEM, sec)] + [(HBM, a) for a in (left_own, left_arrived, lt, opp, x_down, x_up)],
        scratch=[env_scratch, total_scratch]
        + [half_scratch] * 3
        + [pltpu.SemaphoreType.DMA((5,))],
        flops=2 * 36 * 2 * 128**3,
    )

    slots = (OWN, X_OWN, DOWN, UP, OPP, X_DOWN, X_UP)
    pairs = (own, b_x, down, up, opp, x_down, x_up)

    def last(wts, sizes, sec, order, lo, la, lm, ro, ra, rm, lt_in, late0, late1, *rest):
        pairs, rest = rest[: TERMS - 1], rest[TERMS - 1 :]
        left_out, right_out, both, left, right, lt, done_left, done_right = rest[:8]
        blocks0, blocks1, half, sems, late_sems, out_sems = rest[8:]
        first_seg, last_seg = seg_flags()

        def places(site, blocks):
            refs = [pair.at[site] for pair in pairs]
            firsts = [pl.multiple_of(shard_at(slot) * share, share) for slot in slots]
            return [(ref, blocks.at[pl.ds(f, share)]) for ref, f in zip(refs, firsts)]

        first = shard_at(X_OPP) * share
        late = pl.ds(pl.multiple_of(first, share), share)
        left_mid = lax.axis_index("seg") == lax.axis_size("seg") // 2
        plain = jnp.logical_not(jnp.logical_or(first_seg, left_mid))
        edges = ((first_seg, lo), (left_mid, lm), (plain, la))
        for_left = [choose(edges, left, late_sems.at[0])]
        for_left += move([(late0, blocks0.at[late]), (lt_in, lt)], late_sems.at[pl.ds(1, 2)])
        middle = lax.axis_index("seg") == lax.axis_size("seg") // 2 - 1
        plain = jnp.logical_not(jnp.logical_or(last_seg, middle))
        edges = ((last_seg, ro), (middle, rm), (plain, ra))
        copies1 = [choose(edges, right, late_sems.at[3])]
        copies1 += move([(late1, blocks1.at[late])], late_sems.at[pl.ds(4, 1)])
        copies1 += move(places(1, blocks1), sems.at[pl.ds(0, TERMS - 1)])
        wait(for_left)
        copies0 = move(places(0, blocks0), sems.at[pl.ds(TERMS - 1, TERMS - 1)])

        @pl.when(jnp.logical_not(left_mid))
        def _():
            add_left(left, lt, blocks0.at[late], sec, wts, 0, first, share)
            finish(lt, sizes, left)

        wait(copies0)

        @pl.when(left_mid)
        def _():
            left_outward(left, blocks0, half, order, wts, 0, UNROLL)
            left_inward(blocks0, half, keep(left, sizes), order, 0, num, UNROLL)

        wait(copies1)
        sent = []

        def sender(done, out, at):
            def send(begin, end):
                count = (end - begin) // per
                to = both.at[pl.ds(begin // per, count), pl.ds(at * per, per)]
                rows = pl.ds(begin, end - begin)
                packed = done.at[rows].reshape(count, per, width, width)
                going = [(done.at[rows], out.at[rows]), (packed, to)]
                sent.extend(move(going, out_sems.at[pl.ds(len(sent), 2)]))

            return send

        cuts = (0, num // 2)
        left_outward(left, blocks1, half, order, wts, 1, UNROLL)
        left_inward(
            blocks1, half, keep(done_left, sizes), order, 1, num, UNROLL,
            cuts, sender(done_left, left_out, 0),
        )
        right_outward(right, blocks1, half, order, wts, 1, UNROLL)
        right_inward(blocks1, half, keep(right, sizes), order, 1, num, UNROLL)
        right_outward(right, blocks0, half, order, wts, 0, UNROLL)
        right_inward(
            blocks0, half, keep(done_right, sizes), order, 0, num, UNROLL,
            cuts, sender(done_right, right_out, 1),
        )
        wait(sent)

    packed = jax.ShapeDtypeStruct((TERMS, 2 * per, width, width), BF16)
    left_state, right_state, both = call(
        last,
        [(HBM, env), (HBM, env), (HBM, packed)],
        [(SMEM, wts), (SMEM, sector_sizes), (SMEM, sec), (SMEM, order)]
        + [(HBM, a) for a in (left_own, left_arrived, left_middle, right_own, right_arrived, right_middle)]
        + [(HBM, a) for a in (lt, x_opp0, x_opp1)]
        + [(HBM, a) for a in pairs],
        scratch=[env_scratch] * 2
        + [total_scratch]
        + [env_scratch] * 2
        + [site_scratch] * 3
        + [pltpu.SemaphoreType.DMA((2 * TERMS - 2,))]
        + [pltpu.SemaphoreType.DMA((5,)), pltpu.SemaphoreType.DMA((8,))],
        flops=2 * 300 * 2 * 128**3,
        vmem=K_VMEM,
    )
    parts = lax.all_to_all(both, "op", 0, 0, tiled=True)

    def sum_terms(parts, left_sum, right_sum):
        for t in range(per):
            for out, at in ((left_sum, t), (right_sum, per + t)):
                value = parts[0, at].astype(F32)
                for term in range(1, TERMS):
                    value += parts[term, at].astype(F32)
                out[t] = value

    part = jax.ShapeDtypeStruct((per, width, width), F32)
    left_sum, right_sum = call(sum_terms, [(VMEM, part), (VMEM, part)], [(VMEM, parts)], vmem=16)
    return left_state[None, None], right_state[None, None], left_sum[None], right_sum[None]


def solution(mesh):
    placed = (
        P("seg", "op", None, None, None),
        P("seg", "op", None, None, None),
        P("seg", "op", None, None),
        P("seg", None, None),
        P("seg", "op", None),
        P(),
    )
    return jax.shard_map(
        local,
        mesh=mesh,
        in_specs=placed,
        out_specs=(
            P("seg", "op", None, None, None),
            P("seg", "op", None, None, None),
            P("seg", "op", None, None),
            P("seg", "op", None, None),
        ),
        check_vma=False,
    )
```

```python
import jax
import jax.numpy as jnp
from jax import lax
from jax.experimental import pallas as pl
from jax.experimental.pallas import tpu as pltpu
from jax.sharding import PartitionSpec as P

F32 = jnp.float32
BF16 = jnp.bfloat16
VMEM = pl.BlockSpec(memory_space=pltpu.VMEM)
SMEM = pl.BlockSpec(memory_space=pltpu.SMEM)
HBM = pl.BlockSpec(memory_space=pltpu.HBM)
NY, NX = 4, 2
TERMS = NY * NX
PER_SECTOR = 4
UNROLL = 12
K_VMEM = 48
NN = (((1,), (0,)), ((), ()))
TN = (((0,), (0,)), ((), ()))
NT = (((1,), (1,)), ((), ()))
OWN, DOWN, UP, OPP, X_OWN, X_DOWN, X_UP, X_OPP = range(8)
STEPS_OF = ((0, 0), (-1, 0), (1, 0), (2, 0), (0, 1), (-1, 1), (1, 1), (2, 1))


def dot(a, b, dims):
    return lax.dot_general(a, b, dims, preferred_element_type=F32)


def op_route(dy, dx):
    return [(o, ((o // NX + dy) % NY) * NX + ((o % NX) ^ dx)) for o in range(TERMS)]


def hop(block, dy, dx):
    return lax.ppermute(block, "op", op_route(dy, dx))


def along_segments(block, step):
    size = lax.axis_size("seg")
    middle, end = (size // 2 - 1, 0) if step > 0 else (size // 2, size - 1)
    route = [(i, i + step) for i in range(size) if i != middle and 0 <= i + step < size]
    return lax.ppermute(block, "seg", route + [(middle, end)])


def from_ends(block):
    size = lax.axis_size("seg")
    return lax.ppermute(block, "seg", [(0, size // 2), (size - 1, size // 2 - 1)])


def live(sizes, sector, width):
    rows = lax.broadcasted_iota(jnp.int32, (width, width), 0)
    cols = lax.broadcasted_iota(jnp.int32, (width, width), 1)
    return jnp.maximum(rows, cols) < sizes[sector]


def finish(total, sizes, out):
    num, width, _ = total.shape

    @pl.loop(0, num, step=4)
    def _(start):
        for u in range(4):
            alive = live(sizes, start + u, width)
            out[start + u] = jnp.where(alive, total[start + u].astype(F32), 0.0).astype(BF16)


def rank_blocks(sectors, out, n):
    place = lax.broadcasted_iota(jnp.int32, (n, n), 0)
    block = lax.broadcasted_iota(jnp.int32, (n, n), 1)
    earlier = jnp.where(place < block, 1.0, 0.0).astype(BF16)
    index = lax.broadcasted_iota(jnp.int32, (8, n), 1).astype(F32).astype(BF16)
    for site in range(2):
        for side in range(2):
            mine = sectors[site, side : side + 1, :] == place // PER_SECTOR
            seen = dot(jnp.where(mine, 1.0, 0.0).astype(BF16), earlier, NN)
            wanted = (place % PER_SECTOR).astype(F32)
            chosen = jnp.where(jnp.logical_and(mine, seen == wanted), 1.0, 0.0).astype(BF16)
            row = dot(index, chosen, NT)[:1].astype(jnp.int32)
            out[2 * site + side : 2 * site + side + 1, :n] = row


def group(order, table, sector):
    return [order[table, PER_SECTOR * sector + j] for j in range(PER_SECTOR)]


def stage(first, last, unroll, body):
    @pl.loop(first, last, step=unroll)
    def _(start):
        for u in range(unroll):
            body(start + u)


def keep(out, sizes=None):
    def emit(sector, value):
        if sizes is None:
            out[sector] = value
        else:
            alive = live(sizes, sector, value.shape[0])
            out[sector] = jnp.where(alive, value, 0.0).astype(BF16)

    return emit


def left_outward(env, blocks, half, order, weights, site, unroll):
    num, width, _ = env.shape

    def outward(s):
        members = group(order, 2 * site, s)
        found = dot(env[s], jnp.concatenate([blocks[k] for k in members], axis=1), NN)
        for j, k in enumerate(members):
            piece = found[:, j * width : (j + 1) * width]
            half[k] = (piece * weights[site, 0, k]).astype(BF16)

    stage(0, num, unroll, outward)


def left_inward(blocks, half, emit, order, site, num, unroll, cuts=(0,), done=None):
    def inward(t):
        members = group(order, 2 * site + 1, t)
        a = jnp.concatenate([blocks[k] for k in members], axis=0)
        y = jnp.concatenate([half[k] for k in members], axis=0)
        emit(t, dot(a, y, TN))

    in_parts(inward, num, unroll, cuts, done)


def right_outward(env, blocks, half, order, weights, site, unroll):
    num, width, _ = env.shape

    def outward(t):
        members = group(order, 2 * site + 1, t)
        found = dot(jnp.concatenate([blocks[k] for k in members], axis=0), env[t], NN)
        for j, k in enumerate(members):
            piece = found[j * width : (j + 1) * width]
            half[k] = (piece * weights[site, 0, k]).astype(BF16)

    stage(0, num, unroll, outward)


def right_inward(blocks, half, emit, order, site, num, unroll, cuts=(0,), done=None):
    def inward(s):
        members = group(order, 2 * site, s)
        a = jnp.concatenate([blocks[k] for k in members], axis=1)
        z = jnp.concatenate([half[k] for k in members], axis=1)
        emit(s, dot(z, a, NT))

    in_parts(inward, num, unroll, cuts, done)


def in_parts(body, num, unroll, cuts, done):
    for first, last in zip(cuts, tuple(cuts[1:]) + (num,)):
        stage(first, last, min(unroll, last - first), body)
        if done is not None:
            done(first, last)


def add_left(env, total, blocks, sectors, weights, site, first, count):
    found = []
    for j in range(count):
        k = first + j
        block = blocks[j]
        half = (dot(env[sectors[site, 0, k]], block, NN) * weights[site, 0, k]).astype(BF16)
        found.append((sectors[site, 1, k], dot(block, half, TN)))
    for place, value in found:
        total[place] += value


def add_right(env, total, blocks, sectors, weights, site, first, count):
    found = []
    for j in range(count):
        k = first + j
        block = blocks[j]
        half = (dot(block, env[sectors[site, 1, k]], NN) * weights[site, 0, k]).astype(BF16)
        found.append((sectors[site, 0, k], dot(half, block, NT)))
    for place, value in found:
        total[place] += value


def shard_at(slot):
    dy, dx = STEPS_OF[slot]
    me = lax.axis_index("op")
    return ((me // NX + dy + NY) % NY) * NX + ((me % NX) ^ dx)


def after(token, *arrays):
    def body(token, *refs):
        pass

    return pl.pallas_call(
        body,
        out_shape=[jax.ShapeDtypeStruct(a.shape, a.dtype) for a in arrays],
        in_specs=[SMEM] + [HBM] * len(arrays),
        out_specs=[HBM] * len(arrays),
        input_output_aliases={1 + i: i for i in range(len(arrays))},
    )(token, *arrays)


def call(body, outs, ins, scratch=(), flops=0, vmem=48):
    return pl.pallas_call(
        body,
        out_shape=[shape for _, shape in outs],
        in_specs=[spec for spec, _ in ins],
        out_specs=[spec for spec, _ in outs],
        scratch_shapes=list(scratch),
        compiler_params=pltpu.CompilerParams(vmem_limit_bytes=vmem * 1024 * 1024),
        cost_estimate=pl.CostEstimate(flops=flops, bytes_accessed=6000000, transcendentals=0),
    )(*[array for _, array in ins])


def local(left_in, right_in, site_blocks, sectors, site_operator, sector_sizes):
    num, width = left_in.shape[2], left_in.shape[3]
    n = sectors.shape[1]
    share = n // TERMS
    per = num // TERMS
    env = jax.ShapeDtypeStruct((num, width, width), BF16)
    total = jax.ShapeDtypeStruct((num, width, width), F32)
    site_shape = jax.ShapeDtypeStruct((share, width, width), BF16)
    token_shape = jax.ShapeDtypeStruct((1,), jnp.int32)
    env_scratch = pltpu.VMEM(env.shape, BF16)
    total_scratch = pltpu.VMEM(total.shape, F32)
    site_scratch = pltpu.VMEM((n, width, width), BF16)
    sec = jnp.transpose(sectors, (0, 2, 1))
    wts = site_operator

    def move(pairs, sems):
        copies = [
            pltpu.make_async_copy(source, into, sems.at[i])
            for i, (source, into) in enumerate(pairs)
        ]
        for copy in copies:
            copy.start()
        return copies

    def wait(copies):
        for copy in copies:
            copy.wait()

    own = site_blocks
    b_x = hop(own, 0, 1)
    down = hop(own, 1, 0)
    up = hop(own, -1, 0)

    def prepare(sizes, sec_rows, lo_in, ro_in, lo_out, ro_out, order, left, right, ranked, sems):
        coming = move([(lo_in, left), (ro_in, right)], sems.at[pl.ds(0, 2)])
        rank_blocks(sec_rows, ranked, n)
        ranking = move([(ranked, order)], sems.at[pl.ds(2, 1)])
        going = []
        for i, (env_ref, out) in enumerate(((left, lo_out), (right, ro_out))):
            coming[i].wait()
            finish(env_ref, sizes, env_ref)
            going += move([(env_ref, out)], sems.at[pl.ds(3 + i, 1)])
        wait(ranking + going)

    left_own, right_own, order = call(
        prepare,
        [(HBM, env)] * 2 + [(SMEM, jax.ShapeDtypeStruct((4, 128), jnp.int32))],
        [(SMEM, sector_sizes), (VMEM, sec), (HBM, left_in[0, 0]), (HBM, right_in[0, 0])],
        scratch=[env_scratch] * 2
        + [pltpu.VMEM((4, 128), jnp.int32), pltpu.SemaphoreType.DMA((5,))],
    )
    left_arrived = along_segments(left_own, 1)
    right_arrived = along_segments(right_own, -1)
    x_up = hop(b_x, -1, 0)
    x_down = hop(down, 0, 1)
    opp = hop(down, 1, 0)

    def seg_flags():
        seg, size = lax.axis_index("seg"), lax.axis_size("seg")
        return seg == 0, seg == size - 1

    def choose(pairs, into, sem):
        for flag, source in pairs:

            @pl.when(flag)
            def _():
                pltpu.make_async_copy(source, into, sem).start()

        return pltpu.make_async_copy(pairs[0][1], into, sem)

    pair_scratch = pltpu.VMEM((2, share, width, width), BF16)
    half_scratch = pltpu.VMEM((share, width, width), BF16)

    def near(wts, sec, lo, la, ra, own, down, up, b_x, lt_out, token, left, lt, *rest):
        ins, sems, env_sem = rest[:4], rest[4], rest[5]
        first_seg, _ = seg_flags()
        edges = ((first_seg, lo), (jnp.logical_not(first_seg), la))
        coming_left = choose(edges, left, env_sem)
        coming = move([(a.at[0], b) for a, b in zip((own, down, up, b_x), ins)], sems)
        token[0] = 0

        @pl.loop(0, num, step=4)
        def _(t):
            for u in range(4):
                lt[t + u] = jnp.zeros((width, width), F32)

        coming_left.wait()
        for ref, slot, copy in zip(ins, (OWN, DOWN, UP, X_OWN), coming):
            copy.wait()
            add_left(left, lt, ref, sec, wts, 0, shard_at(slot) * share, share)
        wait(move([(lt, lt_out)], sems))

    lt, token = call(
        near,
        [(HBM, total), (SMEM, token_shape)],
        [(SMEM, wts), (SMEM, sec)]
        + [(HBM, a) for a in (left_own, left_arrived, right_arrived, own, down, up, b_x)],
        scratch=[env_scratch, total_scratch]
        + [half_scratch] * 4
        + [pltpu.SemaphoreType.DMA((4,)), pltpu.SemaphoreType.DMA(())],
        flops=2 * 48 * 2 * 128**3,
    )

    def pick(token, x_down, x_up, la, ra, out0, out1, passing, sems):
        first_seg, last_seg = seg_flags()
        coming = move([(x_down.at[0], out0), (x_up.at[1], out1)], sems.at[pl.ds(0, 2)])
        for flag, source in ((first_seg, la), (last_seg, ra)):

            @pl.when(flag)
            def _():
                wait(move([(source, passing)], sems.at[pl.ds(2, 1)]))

        wait(coming)

    send0, send1, passing = call(
        pick,
        [(VMEM, site_shape), (VMEM, site_shape), (VMEM, env)],
        [(SMEM, token)] + [(HBM, a) for a in (x_down, x_up, left_arrived, right_arrived)],
        scratch=[pltpu.SemaphoreType.DMA((3,))],
        vmem=4,
    )
    env_middle = from_ends(passing)
    x_opp0 = hop(send0, 1, 0)
    x_opp1 = hop(send1, -1, 0)

    def further(wts, sec, lo, la, lt_in, opp, x_down, x_up, lt_out, left, lt, *rest):
        ins, sems = rest[:3], rest[3]
        first_seg, _ = seg_flags()
        edges = ((first_seg, lo), (jnp.logical_not(first_seg), la))
        coming = [choose(edges, left, sems.at[0])] + move([(lt_in, lt)], sems.at[pl.ds(1, 1)])
        froms = [a.at[0] for a in (opp, x_down, x_up)]
        blocks = move(list(zip(froms, ins)), sems.at[pl.ds(2, 3)])
        wait(coming)
        for ref, slot, copy in zip(ins, (OPP, X_DOWN, X_UP), blocks):
            copy.wait()
            add_left(left, lt, ref, sec, wts, 0, shard_at(slot) * share, share)
        wait(move([(lt, lt_out)], sems.at[pl.ds(1, 1)]))

    (lt,) = call(
        further,
        [(HBM, total)],
        [(SMEM, wts), (SMEM, sec)] + [(HBM, a) for a in (left_own, left_arrived, lt, opp, x_down, x_up)],
        scratch=[env_scratch, total_scratch]
        + [half_scratch] * 3
        + [pltpu.SemaphoreType.DMA((5,))],
        flops=2 * 36 * 2 * 128**3,
    )

    slots = (OWN, X_OWN, DOWN, UP, OPP, X_DOWN, X_UP)
    pairs = (own, b_x, down, up, opp, x_down, x_up)

    def last(wts, sizes, sec, order, lo, la, ro, ra, mid, lt_in, late0, late1, *rest):
        pairs, rest = rest[: TERMS - 1], rest[TERMS - 1 :]
        left_out, right_out, both, left, right, lt, done_left, done_right = rest[:8]
        blocks0, blocks1, half, sems, late_sems, out_sems = rest[8:]
        first_seg, last_seg = seg_flags()

        def places(site, blocks):
            refs = [pair.at[site] for pair in pairs]
            firsts = [pl.multiple_of(shard_at(slot) * share, share) for slot in slots]
            return [(ref, blocks.at[pl.ds(f, share)]) for ref, f in zip(refs, firsts)]

        first = shard_at(X_OPP) * share
        late = pl.ds(pl.multiple_of(first, share), share)
        left_mid = lax.axis_index("seg") == lax.axis_size("seg") // 2
        plain = jnp.logical_not(jnp.logical_or(first_seg, left_mid))
        edges = ((first_seg, lo), (left_mid, mid), (plain, la))
        for_left = [choose(edges, left, late_sems.at[0])]
        for_left += move([(late0, blocks0.at[late]), (lt_in, lt)], late_sems.at[pl.ds(1, 2)])
        middle = lax.axis_index("seg") == lax.axis_size("seg") // 2 - 1
        plain = jnp.logical_not(jnp.logical_or(last_seg, middle))
        edges = ((last_seg, ro), (middle, mid), (plain, ra))
        copies1 = [choose(edges, right, late_sems.at[3])]
        copies1 += move([(late1, blocks1.at[late])], late_sems.at[pl.ds(4, 1)])
        copies1 += move(places(1, blocks1), sems.at[pl.ds(0, TERMS - 1)])
        wait(for_left)

        @pl.when(jnp.logical_not(left_mid))
        def _():
            add_left(left, lt, blocks0.at[late], sec, wts, 0, first, share)
            finish(lt, sizes, left)

        wait(copies1)
        copies0 = move(places(0, blocks0), sems.at[pl.ds(TERMS - 1, TERMS - 1)])

        @pl.when(left_mid)
        def _():
            wait(copies0)
            left_outward(left, blocks0, half, order, wts, 0, UNROLL)
            left_inward(blocks0, half, keep(left, sizes), order, 0, num, UNROLL)

        sent = []

        def sender(done, out, at):
            def send(begin, end):
                count = (end - begin) // per
                to = both.at[pl.ds(begin // per, count), pl.ds(at * per, per)]
                rows = pl.ds(begin, end - begin)
                packed = done.at[rows].reshape(count, per, width, width)
                going = [(done.at[rows], out.at[rows]), (packed, to)]
                sent.extend(move(going, out_sems.at[pl.ds(len(sent), 2)]))

            return send

        cuts = (0, num // 2)
        left_outward(left, blocks1, half, order, wts, 1, UNROLL)
        left_inward(
            blocks1, half, keep(done_left, sizes), order, 1, num, UNROLL,
            cuts, sender(done_left, left_out, 0),
        )
        right_outward(right, blocks1, half, order, wts, 1, UNROLL)
        right_inward(blocks1, half, keep(right, sizes), order, 1, num, UNROLL)

        @pl.when(jnp.logical_not(left_mid))
        def _():
            wait(copies0)

        right_outward(right, blocks0, half, order, wts, 0, UNROLL)
        right_inward(
            blocks0, half, keep(done_right, sizes), order, 0, num, UNROLL,
            cuts, sender(done_right, right_out, 1),
        )
        wait(sent)

    packed = jax.ShapeDtypeStruct((TERMS, 2 * per, width, width), BF16)
    left_state, right_state, both = call(
        last,
        [(HBM, env), (HBM, env), (HBM, packed)],
        [(SMEM, wts), (SMEM, sector_sizes), (SMEM, sec), (SMEM, order)]
        + [(HBM, a) for a in (left_own, left_arrived, right_own, right_arrived, env_middle)]
        + [(HBM, a) for a in (lt, x_opp0, x_opp1)]
        + [(HBM, a) for a in pairs],
        scratch=[env_scratch] * 2
        + [total_scratch]
        + [env_scratch] * 2
        + [site_scratch] * 3
        + [pltpu.SemaphoreType.DMA((2 * TERMS - 2,))]
        + [pltpu.SemaphoreType.DMA((5,)), pltpu.SemaphoreType.DMA((8,))],
        flops=2 * 300 * 2 * 128**3,
        vmem=K_VMEM,
    )
    parts = lax.all_to_all(both, "op", 0, 0, tiled=True)

    def sum_terms(parts, left_sum, right_sum):
        for t in range(per):
            for out, at in ((left_sum, t), (right_sum, per + t)):
                value = parts[0, at].astype(F32)
                for term in range(1, TERMS):
                    value += parts[term, at].astype(F32)
                out[t] = value

    part = jax.ShapeDtypeStruct((per, width, width), F32)
    left_sum, right_sum = call(sum_terms, [(VMEM, part), (VMEM, part)], [(VMEM, parts)], vmem=16)
    return left_state[None, None], right_state[None, None], left_sum[None], right_sum[None]


def solution(mesh):
    placed = (
        P("seg", "op", None, None, None),
        P("seg", "op", None, None, None),
        P("seg", "op", None, None),
        P("seg", None, None),
        P("seg", "op", None),
        P(),
    )
    return jax.shard_map(
        local,
        mesh=mesh,
        in_specs=placed,
        out_specs=(
            P("seg", "op", None, None, None),
            P("seg", "op", None, None, None),
            P("seg", "op", None, None),
            P("seg", "op", None, None),
        ),
        check_vma=False,
    )
```

```python
import jax
import jax.numpy as jnp
from jax import lax
from jax.experimental import pallas as pl
from jax.experimental.pallas import tpu as pltpu
from jax.sharding import PartitionSpec as P

F32 = jnp.float32
BF16 = jnp.bfloat16
VMEM = pl.BlockSpec(memory_space=pltpu.VMEM)
SMEM = pl.BlockSpec(memory_space=pltpu.SMEM)
HBM = pl.BlockSpec(memory_space=pltpu.HBM)
NY, NX = 4, 2
TERMS = NY * NX
PER_SECTOR = 4
UNROLL = 12
K_VMEM = 48
NN = (((1,), (0,)), ((), ()))
TN = (((0,), (0,)), ((), ()))
NT = (((1,), (1,)), ((), ()))
OWN, DOWN, UP, OPP, X_OWN, X_DOWN, X_UP, X_OPP = range(8)
STEPS_OF = ((0, 0), (-1, 0), (1, 0), (2, 0), (0, 1), (-1, 1), (1, 1), (2, 1))


def dot(a, b, dims):
    return lax.dot_general(a, b, dims, preferred_element_type=F32)


def op_route(dy, dx):
    return [(o, ((o // NX + dy) % NY) * NX + ((o % NX) ^ dx)) for o in range(TERMS)]


def hop(block, dy, dx):
    return lax.ppermute(block, "op", op_route(dy, dx))


def along_segments(block, step):
    size = lax.axis_size("seg")
    middle, end = (size // 2 - 1, 0) if step > 0 else (size // 2, size - 1)
    route = [(i, i + step) for i in range(size) if i != middle and 0 <= i + step < size]
    return lax.ppermute(block, "seg", route + [(middle, end)])


def from_ends(block):
    size = lax.axis_size("seg")
    return lax.ppermute(block, "seg", [(0, size // 2), (size - 1, size // 2 - 1)])


def live(sizes, sector, width):
    rows = lax.broadcasted_iota(jnp.int32, (width, width), 0)
    cols = lax.broadcasted_iota(jnp.int32, (width, width), 1)
    return jnp.maximum(rows, cols) < sizes[sector]


def finish(total, sizes, out):
    num, width, _ = total.shape

    @pl.loop(0, num, step=4)
    def _(start):
        for u in range(4):
            alive = live(sizes, start + u, width)
            out[start + u] = jnp.where(alive, total[start + u].astype(F32), 0.0).astype(BF16)


def rank_blocks(sectors, out, n):
    place = lax.broadcasted_iota(jnp.int32, (n, n), 0)
    block = lax.broadcasted_iota(jnp.int32, (n, n), 1)
    earlier = jnp.where(place < block, 1.0, 0.0).astype(BF16)
    index = lax.broadcasted_iota(jnp.int32, (8, n), 1).astype(F32).astype(BF16)
    for site in range(2):
        for side in range(2):
            mine = sectors[site, side : side + 1, :] == place // PER_SECTOR
            seen = dot(jnp.where(mine, 1.0, 0.0).astype(BF16), earlier, NN)
            wanted = (place % PER_SECTOR).astype(F32)
            chosen = jnp.where(jnp.logical_and(mine, seen == wanted), 1.0, 0.0).astype(BF16)
            row = dot(index, chosen, NT)[:1].astype(jnp.int32)
            out[2 * site + side : 2 * site + side + 1, :n] = row


def group(order, table, sector):
    return [order[table, PER_SECTOR * sector + j] for j in range(PER_SECTOR)]


def stage(first, last, unroll, body):
    @pl.loop(first, last, step=unroll)
    def _(start):
        for u in range(unroll):
            body(start + u)


def keep(out, sizes=None):
    def emit(sector, value):
        if sizes is None:
            out[sector] = value
        else:
            alive = live(sizes, sector, value.shape[0])
            out[sector] = jnp.where(alive, value, 0.0).astype(BF16)

    return emit


def left_outward(env, blocks, half, order, weights, site, unroll):
    num, width, _ = env.shape

    def outward(s):
        members = group(order, 2 * site, s)
        found = dot(env[s], jnp.concatenate([blocks[k] for k in members], axis=1), NN)
        for j, k in enumerate(members):
            piece = found[:, j * width : (j + 1) * width]
            half[k] = (piece * weights[site, 0, k]).astype(BF16)

    stage(0, num, unroll, outward)


def left_inward(blocks, half, emit, order, site, num, unroll, cuts=(0,), done=None):
    def inward(t):
        members = group(order, 2 * site + 1, t)
        a = jnp.concatenate([blocks[k] for k in members], axis=0)
        y = jnp.concatenate([half[k] for k in members], axis=0)
        emit(t, dot(a, y, TN))

    in_parts(inward, num, unroll, cuts, done)


def right_outward(env, blocks, half, order, weights, site, unroll):
    num, width, _ = env.shape

    def outward(t):
        members = group(order, 2 * site + 1, t)
        found = dot(jnp.concatenate([blocks[k] for k in members], axis=0), env[t], NN)
        for j, k in enumerate(members):
            piece = found[j * width : (j + 1) * width]
            half[k] = (piece * weights[site, 0, k]).astype(BF16)

    stage(0, num, unroll, outward)


def right_inward(blocks, half, emit, order, site, num, unroll, cuts=(0,), done=None):
    def inward(s):
        members = group(order, 2 * site, s)
        a = jnp.concatenate([blocks[k] for k in members], axis=1)
        z = jnp.concatenate([half[k] for k in members], axis=1)
        emit(s, dot(z, a, NT))

    in_parts(inward, num, unroll, cuts, done)


def in_parts(body, num, unroll, cuts, done):
    for first, last in zip(cuts, tuple(cuts[1:]) + (num,)):
        stage(first, last, min(unroll, last - first), body)
        if done is not None:
            done(first, last)


def add_left(env, total, blocks, sectors, weights, site, first, count):
    found = []
    for j in range(count):
        k = first + j
        block = blocks[j]
        half = (dot(env[sectors[site, 0, k]], block, NN) * weights[site, 0, k]).astype(BF16)
        found.append((sectors[site, 1, k], dot(block, half, TN)))
    for place, value in found:
        total[place] += value


def add_right(env, total, blocks, sectors, weights, site, first, count):
    found = []
    for j in range(count):
        k = first + j
        block = blocks[j]
        half = (dot(block, env[sectors[site, 1, k]], NN) * weights[site, 0, k]).astype(BF16)
        found.append((sectors[site, 0, k], dot(half, block, NT)))
    for place, value in found:
        total[place] += value


def shard_at(slot):
    dy, dx = STEPS_OF[slot]
    me = lax.axis_index("op")
    return ((me // NX + dy + NY) % NY) * NX + ((me % NX) ^ dx)


def after(token, *arrays):
    def body(token, *refs):
        pass

    return pl.pallas_call(
        body,
        out_shape=[jax.ShapeDtypeStruct(a.shape, a.dtype) for a in arrays],
        in_specs=[SMEM] + [HBM] * len(arrays),
        out_specs=[HBM] * len(arrays),
        input_output_aliases={1 + i: i for i in range(len(arrays))},
    )(token, *arrays)


def call(body, outs, ins, scratch=(), flops=0, vmem=48):
    return pl.pallas_call(
        body,
        out_shape=[shape for _, shape in outs],
        in_specs=[spec for spec, _ in ins],
        out_specs=[spec for spec, _ in outs],
        scratch_shapes=list(scratch),
        compiler_params=pltpu.CompilerParams(vmem_limit_bytes=vmem * 1024 * 1024),
        cost_estimate=pl.CostEstimate(flops=flops, bytes_accessed=6000000, transcendentals=0),
    )(*[array for _, array in ins])


def local(left_in, right_in, site_blocks, sectors, site_operator, sector_sizes):
    num, width = left_in.shape[2], left_in.shape[3]
    n = sectors.shape[1]
    share = n // TERMS
    per = num // TERMS
    env = jax.ShapeDtypeStruct((num, width, width), BF16)
    total = jax.ShapeDtypeStruct((num, width, width), F32)
    site_shape = jax.ShapeDtypeStruct((share, width, width), BF16)
    token_shape = jax.ShapeDtypeStruct((1,), jnp.int32)
    env_scratch = pltpu.VMEM(env.shape, BF16)
    total_scratch = pltpu.VMEM(total.shape, F32)
    site_scratch = pltpu.VMEM((n, width, width), BF16)
    sec = jnp.transpose(sectors, (0, 2, 1))
    wts = site_operator

    def move(pairs, sems):
        copies = [
            pltpu.make_async_copy(source, into, sems.at[i])
            for i, (source, into) in enumerate(pairs)
        ]
        for copy in copies:
            copy.start()
        return copies

    def wait(copies):
        for copy in copies:
            copy.wait()

    own = site_blocks
    b_x = hop(own, 0, 1)
    down = hop(own, 1, 0)
    up = hop(own, -1, 0)

    def prepare(sizes, sec_rows, lo_in, ro_in, lo_out, ro_out, order, left, right, ranked, sems):
        coming = move([(lo_in, left), (ro_in, right)], sems.at[pl.ds(0, 2)])
        rank_blocks(sec_rows, ranked, n)
        ranking = move([(ranked, order)], sems.at[pl.ds(2, 1)])
        going = []
        for i, (env_ref, out) in enumerate(((left, lo_out), (right, ro_out))):
            coming[i].wait()
            finish(env_ref, sizes, env_ref)
            going += move([(env_ref, out)], sems.at[pl.ds(3 + i, 1)])
        wait(ranking + going)

    left_own, right_own, order = call(
        prepare,
        [(HBM, env)] * 2 + [(SMEM, jax.ShapeDtypeStruct((4, 128), jnp.int32))],
        [(SMEM, sector_sizes), (VMEM, sec), (HBM, left_in[0, 0]), (HBM, right_in[0, 0])],
        scratch=[env_scratch] * 2
        + [pltpu.VMEM((4, 128), jnp.int32), pltpu.SemaphoreType.DMA((5,))],
    )
    left_arrived = along_segments(left_own, 1)
    right_arrived = along_segments(right_own, -1)
    x_up = hop(b_x, -1, 0)
    x_down = hop(down, 0, 1)
    opp = hop(down, 1, 0)

    def seg_flags():
        seg, size = lax.axis_index("seg"), lax.axis_size("seg")
        return seg == 0, seg == size - 1

    def choose(pairs, into, sem):
        for flag, source in pairs:

            @pl.when(flag)
            def _():
                pltpu.make_async_copy(source, into, sem).start()

        return pltpu.make_async_copy(pairs[0][1], into, sem)

    pair_scratch = pltpu.VMEM((2, share, width, width), BF16)
    half_scratch = pltpu.VMEM((share, width, width), BF16)

    def near(wts, sec, lo, la, ra, own, down, up, b_x, lt_out, token, left, lt, *rest):
        ins, sems, env_sem = rest[:4], rest[4], rest[5]
        first_seg, _ = seg_flags()
        edges = ((first_seg, lo), (jnp.logical_not(first_seg), la))
        coming_left = choose(edges, left, env_sem)
        coming = move([(a.at[0], b) for a, b in zip((own, down, up, b_x), ins)], sems)
        token[0] = 0

        @pl.loop(0, num, step=4)
        def _(t):
            for u in range(4):
                lt[t + u] = jnp.zeros((width, width), F32)

        coming_left.wait()
        for ref, slot, copy in zip(ins, (OWN, DOWN, UP, X_OWN), coming):
            copy.wait()
            add_left(left, lt, ref, sec, wts, 0, shard_at(slot) * share, share)
        wait(move([(lt, lt_out)], sems))

    lt, token = call(
        near,
        [(HBM, total), (SMEM, token_shape)],
        [(SMEM, wts), (SMEM, sec)]
        + [(HBM, a) for a in (left_own, left_arrived, right_arrived, own, down, up, b_x)],
        scratch=[env_scratch, total_scratch]
        + [half_scratch] * 4
        + [pltpu.SemaphoreType.DMA((4,)), pltpu.SemaphoreType.DMA(())],
        flops=2 * 48 * 2 * 128**3,
    )

    def pick_up(token, x_up, out, sems):
        wait(move([(x_up.at[1], out)], sems))

    (send1,) = call(
        pick_up,
        [(VMEM, site_shape)],
        [(SMEM, token), (HBM, x_up)],
        scratch=[pltpu.SemaphoreType.DMA((1,))],
        vmem=4,
    )

    def pick_down(token, x_down, la, ra, out, passing, sems):
        first_seg, last_seg = seg_flags()
        coming = move([(x_down.at[0], out)], sems.at[pl.ds(0, 1)])
        for flag, source in ((first_seg, la), (last_seg, ra)):

            @pl.when(flag)
            def _():
                wait(move([(source, passing)], sems.at[pl.ds(1, 1)]))

        wait(coming)

    send0, passing = call(
        pick_down,
        [(VMEM, site_shape), (VMEM, env)],
        [(SMEM, token)] + [(HBM, a) for a in (x_down, left_arrived, right_arrived)],
        scratch=[pltpu.SemaphoreType.DMA((2,))],
        vmem=4,
    )
    env_middle = from_ends(passing)
    x_opp0 = hop(send0, 1, 0)
    x_opp1 = hop(send1, -1, 0)

    def further(wts, sec, lo, la, lt_in, opp, x_down, x_up, lt_out, left, lt, *rest):
        ins, sems = rest[:3], rest[3]
        first_seg, _ = seg_flags()
        edges = ((first_seg, lo), (jnp.logical_not(first_seg), la))
        coming = [choose(edges, left, sems.at[0])] + move([(lt_in, lt)], sems.at[pl.ds(1, 1)])
        froms = [a.at[0] for a in (opp, x_down, x_up)]
        blocks = move(list(zip(froms, ins)), sems.at[pl.ds(2, 3)])
        wait(coming)
        for ref, slot, copy in zip(ins, (OPP, X_DOWN, X_UP), blocks):
            copy.wait()
            add_left(left, lt, ref, sec, wts, 0, shard_at(slot) * share, share)
        wait(move([(lt, lt_out)], sems.at[pl.ds(1, 1)]))

    (lt,) = call(
        further,
        [(HBM, total)],
        [(SMEM, wts), (SMEM, sec)] + [(HBM, a) for a in (left_own, left_arrived, lt, opp, x_down, x_up)],
        scratch=[env_scratch, total_scratch]
        + [half_scratch] * 3
        + [pltpu.SemaphoreType.DMA((5,))],
        flops=2 * 36 * 2 * 128**3,
    )

    slots = (OWN, X_OWN, DOWN, UP, OPP, X_DOWN, X_UP)
    pairs = (own, b_x, down, up, opp, x_down, x_up)

    def last(wts, sizes, sec, order, lo, la, ro, ra, mid, lt_in, late0, late1, *rest):
        pairs, rest = rest[: TERMS - 1], rest[TERMS - 1 :]
        left_out, right_out, both, left, right, lt, done_left, done_right = rest[:8]
        blocks0, blocks1, half, sems, late_sems, out_sems = rest[8:]
        first_seg, last_seg = seg_flags()

        def places(site, blocks):
            refs = [pair.at[site] for pair in pairs]
            firsts = [pl.multiple_of(shard_at(slot) * share, share) for slot in slots]
            return [(ref, blocks.at[pl.ds(f, share)]) for ref, f in zip(refs, firsts)]

        first = shard_at(X_OPP) * share
        late = pl.ds(pl.multiple_of(first, share), share)
        left_mid = lax.axis_index("seg") == lax.axis_size("seg") // 2
        plain = jnp.logical_not(jnp.logical_or(first_seg, left_mid))
        edges = ((first_seg, lo), (left_mid, mid), (plain, la))
        for_left = [choose(edges, left, late_sems.at[0])]
        for_left += move([(late0, blocks0.at[late]), (lt_in, lt)], late_sems.at[pl.ds(1, 2)])
        middle = lax.axis_index("seg") == lax.axis_size("seg") // 2 - 1
        plain = jnp.logical_not(jnp.logical_or(last_seg, middle))
        edges = ((last_seg, ro), (middle, mid), (plain, ra))
        copies1 = [choose(edges, right, late_sems.at[3])]
        copies1 += move([(late1, blocks1.at[late])], late_sems.at[pl.ds(4, 1)])
        copies1 += move(places(1, blocks1), sems.at[pl.ds(0, TERMS - 1)])
        wait(for_left)

        @pl.when(jnp.logical_not(left_mid))
        def _():
            add_left(left, lt, blocks0.at[late], sec, wts, 0, first, share)
            finish(lt, sizes, left)

        wait(copies1)
        copies0 = move(places(0, blocks0), sems.at[pl.ds(TERMS - 1, TERMS - 1)])

        @pl.when(left_mid)
        def _():
            wait(copies0)
            left_outward(left, blocks0, half, order, wts, 0, UNROLL)
            left_inward(blocks0, half, keep(left, sizes), order, 0, num, UNROLL)

        sent = []

        def sender(done, out, at):
            def send(begin, end):
                count = (end - begin) // per
                to = both.at[pl.ds(begin // per, count), pl.ds(at * per, per)]
                rows = pl.ds(begin, end - begin)
                packed = done.at[rows].reshape(count, per, width, width)
                going = [(done.at[rows], out.at[rows]), (packed, to)]
                sent.extend(move(going, out_sems.at[pl.ds(len(sent), 2)]))

            return send

        cuts = (0, num // 2)
        left_outward(left, blocks1, half, order, wts, 1, UNROLL)
        left_inward(
            blocks1, half, keep(done_left, sizes), order, 1, num, UNROLL,
            cuts, sender(done_left, left_out, 0),
        )
        right_outward(right, blocks1, half, order, wts, 1, UNROLL)
        right_inward(blocks1, half, keep(right, sizes), order, 1, num, UNROLL)

        @pl.when(jnp.logical_not(left_mid))
        def _():
            wait(copies0)

        right_outward(right, blocks0, half, order, wts, 0, UNROLL)
        right_inward(
            blocks0, half, keep(done_right, sizes), order, 0, num, UNROLL,
            cuts, sender(done_right, right_out, 1),
        )
        wait(sent)

    packed = jax.ShapeDtypeStruct((TERMS, 2 * per, width, width), BF16)
    left_state, right_state, both = call(
        last,
        [(HBM, env), (HBM, env), (HBM, packed)],
        [(SMEM, wts), (SMEM, sector_sizes), (SMEM, sec), (SMEM, order)]
        + [(HBM, a) for a in (left_own, left_arrived, right_own, right_arrived, env_middle)]
        + [(HBM, a) for a in (lt, x_opp0, x_opp1)]
        + [(HBM, a) for a in pairs],
        scratch=[env_scratch] * 2
        + [total_scratch]
        + [env_scratch] * 2
        + [site_scratch] * 3
        + [pltpu.SemaphoreType.DMA((2 * TERMS - 2,))]
        + [pltpu.SemaphoreType.DMA((5,)), pltpu.SemaphoreType.DMA((8,))],
        flops=2 * 300 * 2 * 128**3,
        vmem=K_VMEM,
    )
    parts = lax.all_to_all(both, "op", 0, 0, tiled=True)

    def sum_terms(parts, left_sum, right_sum):
        for t in range(per):
            for out, at in ((left_sum, t), (right_sum, per + t)):
                value = parts[0, at].astype(F32)
                for term in range(1, TERMS):
                    value += parts[term, at].astype(F32)
                out[t] = value

    part = jax.ShapeDtypeStruct((per, width, width), F32)
    left_sum, right_sum = call(sum_terms, [(VMEM, part), (VMEM, part)], [(VMEM, parts)], vmem=16)
    return left_state[None, None], right_state[None, None], left_sum[None], right_sum[None]


def solution(mesh):
    placed = (
        P("seg", "op", None, None, None),
        P("seg", "op", None, None, None),
        P("seg", "op", None, None),
        P("seg", None, None),
        P("seg", "op", None),
        P(),
    )
    return jax.shard_map(
        local,
        mesh=mesh,
        in_specs=placed,
        out_specs=(
            P("seg", "op", None, None, None),
            P("seg", "op", None, None, None),
            P("seg", "op", None, None),
            P("seg", "op", None, None),
        ),
        check_vma=False,
    )
```
